128 devices in a mesh: sx: 16 (over z_hi, y, core), sy: 8 (over x, z_lo).
Axes of the slice: x: 4, y: 4, z: 4 (z_hi: 2, z_lo: 2; z = z_hi * 2 + z_lo), core: 2. Of those that a mesh axis runs over, the one named last changes fastest.
Arguments:
- vectors: bfloat16 [64, 128, 256, 128], P(None, 'sx', 'sy'), may hold values from -0.4453125 to 0.4453125
- root_stiff: float32 [128, 256, 128], P('sx', 'sy'), may hold values from 0.5 to 2
- diag_coef: float32 [128, 256, 128], P('sx', 'sy'), may hold values from -3 to 3
- counts: int32 [16, 8], P('sx', 'sy'), may hold values from 8 to 64, as said below
Outputs:
- own_block: float32 [16, 8, 64, 64], P('sx', 'sy')
- face_blocks: float32 [16, 8, 64, 256], P('sx', 'sy')
- corner_blocks: float32 [16, 8, 64, 256], P('sx', 'sy')
- offsets: int32 [16, 8], P('sx', 'sy')
The draws below stay inside these ranges and needn't reach their ends.
Inputs may be any that keep to these rules, and one draw needn't show every extreme that they name: Some subdomain has exactly 64 eigenvectors in every draw; small counts are more common than large ones.
All inputs are finite; a program needn't handle non-finite values.
Results may differ from the reference program's by a relative error of at most 0.007.
Values may be sent and summed in bfloat16 or wider, within the bound.
A program may use at most 128 MiB of HBM per device.

```python
import math
import jax
import jax.numpy as jnp
from jax import lax

KMAX = 64
KMIN = 8
CX = 8
CY = 32
CZ = 128
SUB_X = 16
SUB_Y = 8
NX = 128
NY = 256
N_SX = 16
N_SY = 8


def draw_counts(key, part):
    key_one, key_two, key_three = jax.random.split(jax.random.fold_in(key, 11), 3)
    spread = KMAX - KMIN
    draw_one = jax.random.randint(key_one, (N_SX, N_SY), 0, spread + 1)
    draw_two = jax.random.randint(key_two, (N_SX, N_SY), 0, spread + 1)
    skewed = KMIN + draw_one * draw_two // max(spread, 1)
    chosen = jax.random.randint(key_three, (), 0, N_SX * N_SY)
    linear = skewed.reshape(-1)
    linear = jnp.where(jnp.arange(N_SX * N_SY) == chosen, KMAX, linear)
    return linear.reshape(N_SX, N_SY).astype(jnp.int32)


def shard_levels(own_key, shape, cuts, low, largest):
    gain, own = 1.0, jax.random.fold_in(own_key, 6)
    for position, parts in cuts:
        steps = jnp.exp(jax.random.uniform(jax.random.fold_in(own, position), (parts,), jnp.float32, low / len(cuts), largest / len(cuts)))
        gain = gain * jnp.repeat(steps, shape[position] // parts).reshape([-1 if axis == position else 1 for axis in range(len(shape))])
    return gain


def bell_draw(own_key, extent, width, bound, pieces=(), kind=jnp.bfloat16):
    loudness = shard_levels(own_key, extent, pieces, -0.22, 0.18) if pieces else 1.0
    values = jax.random.normal(own_key, extent, jnp.float32) * width * loudness
    return jnp.minimum(jnp.maximum(values, -bound), bound).astype(kind)


def setup_inputs(seed: int = 0) -> dict:
    seeds = jax.random.split(jax.random.key(seed), 5)
    vectors = bell_draw(seeds[0], (KMAX, NX, NY, CZ), (1.0 / (CX * CY * CZ) ** 0.25), 0.4453125, ((1, 16), (2, 8)))
    root_stiff = jnp.clip(jnp.exp(math.log(2.0) - 1.3862944 * jax.random.uniform(seeds[1], (NX, NY, CZ), jnp.float32) ** shard_levels(seeds[1], (NX, NY, CZ), ((0, 16), (1, 8)), -0.2, 0.2)), 0.5, 2.0)
    diag_coef = jnp.clip(jax.random.uniform(seeds[2], (NX, NY, CZ), jnp.float32, -3.0, 3.0) * shard_levels(seeds[2], (NX, NY, CZ), ((0, 16), (1, 8)), -0.4, 0.0), -3.0, 3.0)
    counts = draw_counts(jax.random.fold_in(seeds[4], 71), 0)
    return {"vectors": vectors, "root_stiff": root_stiff, "diag_coef": diag_coef, "counts": counts}


def smooth_along(values, dim_index):
    length = values.shape[dim_index]
    zero_slab = jnp.zeros_like(lax.slice_in_dim(values, 0, 1, axis=dim_index))
    below_side = jnp.concatenate([zero_slab, lax.slice_in_dim(values, 0, length - 1, axis=dim_index)], axis=dim_index)
    above_side = jnp.concatenate([lax.slice_in_dim(values, 1, length, axis=dim_index), zero_slab], axis=dim_index)
    return values + 0.5 * (below_side + above_side)


def own_term(masked, scaled, stiff_here, diag_here):
    scaled_wide = scaled.astype(jnp.float32)
    smoothed = smooth_along(smooth_along(smooth_along(scaled_wide, 1), 2), 3)
    beside = smoothed - scaled_wide
    applied = (diag_here[None] * masked.astype(jnp.float32) - stiff_here[None] * beside).astype(jnp.bfloat16)
    vec_rows = masked.shape[0]
    return lax.dot_general(masked.reshape(vec_rows, -1), applied.reshape(vec_rows, -1), (((1,), (1,)), ((), ())), preferred_element_type=jnp.float32)


def face_term(own_layer, near_layer):
    weighted = 0.5 * smooth_along(smooth_along(near_layer.astype(jnp.float32), 1), 2)
    vec_rows = own_layer.shape[0]
    return -lax.dot_general(own_layer.astype(jnp.float32).reshape(vec_rows, -1), weighted.reshape(vec_rows, -1), (((1,), (1,)), ((), ())), precision=lax.Precision.HIGHEST, preferred_element_type=jnp.float32)


def corner_term(own_column, near_column):
    weighted = 0.25 * smooth_along(near_column.astype(jnp.float32), 1)
    return -lax.dot_general(own_column.astype(jnp.float32), weighted, (((1,), (1,)), ((), ())), precision=lax.Precision.HIGHEST, preferred_element_type=jnp.float32)


def reference(vectors, root_stiff, diag_coef, counts):
    vec_rows = vectors.shape[0]

    def scaled_piece(sub_x, sub_y, x_start, x_len, y_start, y_len):
        inside = (sub_x >= 0) & (sub_x < SUB_X) & (sub_y >= 0) & (sub_y < SUB_Y)
        clamp_x = jnp.clip(sub_x, 0, SUB_X - 1).astype(jnp.int32)
        clamp_y = jnp.clip(sub_y, 0, SUB_Y - 1).astype(jnp.int32)
        start_x = (clamp_x * CX + x_start).astype(jnp.int32)
        start_y = (clamp_y * CY + y_start).astype(jnp.int32)
        zero_start = jnp.zeros((), jnp.int32)
        piece = lax.dynamic_slice(vectors, (zero_start, start_x, start_y, zero_start), (vec_rows, x_len, y_len, CZ))
        stiff = lax.dynamic_slice(root_stiff, (start_x, start_y, zero_start), (x_len, y_len, CZ))
        live_count = counts[clamp_x, clamp_y]
        row_index = lax.broadcasted_iota(jnp.int32, (vec_rows, 1, 1, 1), 0)
        keep = (row_index < live_count) & inside
        masked = jnp.where(keep, piece, jnp.zeros_like(piece))
        scaled = (stiff[None] * masked.astype(jnp.float32)).astype(jnp.bfloat16)
        return masked, scaled, stiff

    def one_subdomain(flat_index):
        sub_x = flat_index // SUB_Y
        sub_y = flat_index % SUB_Y
        masked, scaled, stiff_here = scaled_piece(sub_x, sub_y, 0, CX, 0, CY)
        zero_start = jnp.zeros((), jnp.int32)
        diag_here = lax.dynamic_slice(diag_coef, ((sub_x * CX).astype(jnp.int32), (sub_y * CY).astype(jnp.int32), zero_start), (CX, CY, CZ))
        own_block = own_term(masked, scaled, stiff_here, diag_here)
        faces = []
        for step_x in (-1, 1):
            own_layer = scaled[:, CX - 1 if step_x > 0 else 0]
            near_layer = scaled_piece(sub_x + step_x, sub_y, 0 if step_x > 0 else CX - 1, 1, 0, CY)[1][:, 0]
            faces.append(face_term(own_layer, near_layer))
        for step_y in (-1, 1):
            own_layer = scaled[:, :, CY - 1 if step_y > 0 else 0]
            near_layer = scaled_piece(sub_x, sub_y + step_y, 0, CX, 0 if step_y > 0 else CY - 1, 1)[1][:, :, 0]
            faces.append(face_term(own_layer, near_layer))
        corners = []
        for step_x in (-1, 1):
            for step_y in (-1, 1):
                own_column = scaled[:, CX - 1 if step_x > 0 else 0, CY - 1 if step_y > 0 else 0]
                near_column = scaled_piece(sub_x + step_x, sub_y + step_y, 0 if step_x > 0 else CX - 1, 1, 0 if step_y > 0 else CY - 1, 1)[1][:, 0, 0]
                corners.append(corner_term(own_column, near_column))
        return own_block, jnp.concatenate(faces, axis=1), jnp.concatenate(corners, axis=1)

    own_all, face_all, corner_all = lax.map(one_subdomain, jnp.arange(SUB_X * SUB_Y, dtype=jnp.int32))
    offsets = (jnp.cumsum(counts, axis=1) - counts).astype(jnp.int32)
    return (own_all.reshape(SUB_X, SUB_Y, vec_rows, vec_rows), face_all.reshape(SUB_X, SUB_Y, vec_rows, 4 * vec_rows), corner_all.reshape(SUB_X, SUB_Y, vec_rows, 4 * vec_rows), offsets)
```

```python
import functools

import jax
import jax.numpy as jnp
from jax import lax
from jax.experimental import pallas as pl
from jax.experimental.pallas import tpu as pltpu
from jax.sharding import PartitionSpec as P

MESH = pl.DeviceIdType.MESH
F32 = jnp.float32
BF16 = jnp.bfloat16
CHUNK = 4


def row_dot(left, right):
    return lax.dot_general(left, right, (((1,), (1,)), ((), ())), preferred_element_type=F32)


def along_lanes(pieces):
    return jnp.concatenate(pieces, axis=1)


def block_dot(left_ref, left_start, right_ref, right_start, count):
    return row_dot(
        along_lanes([left_ref[left_start + i] for i in range(count)]),
        along_lanes([right_ref[right_start + i] for i in range(count)]),
    )


def kernel(
    n_x,
    n_y,
    vec_ref,
    rs_ref,
    dg_ref,
    cnt_ref,
    own_ref,
    face_ref,
    corner_ref,
    off_ref,
    vv,
    rs,
    dg,
    wide,
    mb,
    sb,
    zp,
    ab,
    vx,
    vy,
    sy0,
    rxm,
    rxp,
    rym,
    ryp,
    rc,
    pout,
    pin,
    cb,
    cr,
    load_sem,
    send_sem,
    recv_sem,
    csend_sem,
    crecv_sem,
):
    rows, c_x, c_y, c_z = vec_ref.shape
    half_x, half_y = c_x // 2, c_y // 2
    ix, iy = lax.axis_index("sx"), lax.axis_index("sy")

    order = [0, c_x - 1] + list(range(1, c_x - 1))
    loads = {x: pltpu.make_async_copy(vec_ref.at[:, x], vv.at[x], load_sem.at[x]) for x in order}
    rs_load = pltpu.make_async_copy(rs_ref, rs, load_sem.at[c_x])
    dg_load = pltpu.make_async_copy(dg_ref, dg, load_sem.at[c_x + 1])
    loads[0].start()
    rs_load.start()
    loads[c_x - 1].start()
    for x in order[2:]:
        loads[x].start()
    dg_load.start()

    low_x, high_x = ix > 0, ix < n_x - 1
    low_y, high_y = iy > 0, iy < n_y - 1
    faces = [
        (low_x, (ix - 1, iy)),
        (high_x, (ix + 1, iy)),
        (low_y, (ix, iy - 1)),
        (high_y, (ix, iy + 1)),
    ]
    diagonals = [
        (low_x & low_y, (ix - 1, iy - 1)),
        (low_x & high_y, (ix - 1, iy + 1)),
        (high_x & low_y, (ix + 1, iy - 1)),
        (high_x & high_y, (ix + 1, iy + 1)),
    ]

    barrier = pltpu.get_barrier_semaphore()
    for there, device in faces + diagonals:

        @pl.when(there)
        def _(device=device):
            pl.semaphore_signal(barrier, inc=1, device_id=device, device_id_type=MESH)

    for far in range(2, n_y):

        @pl.when(iy >= far)
        def _(far=far):
            pl.semaphore_signal(barrier, inc=1, device_id=(ix, iy - far), device_id_type=MESH)

    beside = sum(there.astype(jnp.int32) for there, _ in faces + diagonals)
    later = jnp.maximum(n_y - 2 - iy, 0)

    count = cnt_ref[0, 0]
    cb[...] = jnp.full(cb.shape, count, jnp.int32)
    keep = lax.broadcasted_iota(jnp.int32, (rows, c_z), 0) < count
    lane_r = lax.broadcasted_iota(jnp.int32, (c_z, c_z), 0)
    lane_c = lax.broadcasted_iota(jnp.int32, (c_z, c_z), 1)
    apart = jnp.abs(lane_r - lane_c)
    smooth = jnp.where(apart == 0, 1.0, jnp.where(apart == 1, 0.5, 0.0)).astype(BF16)

    def zero_slab(x):
        def step(y, _):
            zp[x, y] = jnp.zeros((rows, c_z), F32)
            return _

        lax.fori_loop(0, c_y + 2, step, 0)

    zero_slab(0)
    zero_slab(c_x + 1)
    for x in range(1, c_x + 1):
        zp[x, 0] = jnp.zeros((rows, c_z), F32)
        zp[x, c_y + 1] = jnp.zeros((rows, c_z), F32)

    def widen(x):
        wide[...] = vv[x].reshape(rows * c_y, c_z).astype(F32)

    def scale(x):
        def step(i, _):
            pieces = []
            for j in range(CHUNK):
                y = i * CHUNK + j
                m = wide[pl.ds(y, rows, stride=c_y), :]
                m = jnp.where(keep, m, 0.0)
                s = (m * rs[x, pl.ds(y, 1), :]).astype(BF16)
                mb[x, y] = m.astype(BF16)
                sb[x, y] = s
                pieces.append(s)
            z = jnp.dot(jnp.concatenate(pieces, axis=0), smooth, preferred_element_type=F32)
            for j in range(CHUNK):
                zp[x + 1, i * CHUNK + j + 1] = z[j * rows : (j + 1) * rows]
            return _

        lax.fori_loop(0, c_y // CHUNK, step, 0)

    rs_load.wait()
    for x in (0, c_x - 1):
        loads[x].wait()
        widen(x)
        scale(x)

    def face_step(y, _):
        vx[y] = (-0.25 * ((zp[c_x, y] + zp[c_x, y + 2]) + 2.0 * zp[c_x, y + 1])).astype(BF16)
        return _

    lax.fori_loop(0, c_y, face_step, 0)

    pl.semaphore_wait(barrier, beside + later)

    def to_face(d, phase, to=None):
        opposite = d ^ 1
        if phase == 0:
            src, dst = [
                (sb.at[0, pl.ds(0, half_y)], rxp),
                (vx.at[pl.ds(half_y, half_y)], rxm),
                (sy0.at[pl.ds(0, half_x)], ryp),
                (vy.at[pl.ds(half_x, half_x)], rym),
            ][d]
        else:
            src, dst = pout.at[d], pin.at[opposite]
        return pltpu.make_async_remote_copy(
            src_ref=src,
            dst_ref=dst,
            send_sem=send_sem.at[phase * 4 + d],
            recv_sem=recv_sem.at[phase * 4 + opposite],
            device_id=faces[d if to is None else to][1],
            device_id_type=MESH,
        )

    def from_face(d, phase):
        return to_face(d ^ 1, phase, d)

    def from_corner(d):
        return to_corner(3 - d, d)

    def to_corner(d, to=None):
        opposite = 3 - d
        x, y = (0, c_x - 1)[d // 2], (0, c_y - 1)[d % 2]
        return pltpu.make_async_remote_copy(
            src_ref=sb.at[x, y],
            dst_ref=rc.at[opposite],
            send_sem=send_sem.at[8 + d],
            recv_sem=recv_sem.at[8 + opposite],
            device_id=diagonals[d if to is None else to][1],
            device_id_type=MESH,
        )

    def to_peer(far):
        return pltpu.make_async_remote_copy(
            src_ref=cb,
            dst_ref=cr.at[far],
            send_sem=csend_sem.at[far],
            recv_sem=crecv_sem.at[far],
            device_id=(ix, iy + far),
            device_id_type=MESH,
        )

    def guarded(there, action):
        @pl.when(there)
        def _():
            action()

    for d in (1, 0):
        guarded(faces[d][0], lambda d=d: to_face(d, 0).start())
    for d in range(4):
        guarded(diagonals[d][0], lambda d=d: to_corner(d).start())
    for far in range(1, n_y):
        guarded(iy + far < n_y, lambda far=far: to_peer(far).start())

    for x in order[2:]:
        loads[x].wait()
        widen(x)
        scale(x)

    for x in range(c_x):
        vy[x] = (
            -0.25 * ((zp[x, c_y] + zp[x + 2, c_y]) + 2.0 * zp[x + 1, c_y])
        ).astype(BF16)
        sy0[x] = sb[x, 0]
    for d in (3, 2):
        guarded(faces[d][0], lambda d=d: to_face(d, 0).start())

    dg_load.wait()
    dg[...] = dg[...] + rs[...] * rs[...]
    rs[...] = rs[...] * 0.25

    def apply_slab(x, total):
        def across(y):
            near = zp[x + 1, y]
            return (zp[x, y] + near) + (near + zp[x + 2, y])

        def step(i, carry):
            g_here, u_before, total = carry
            for j in range(CHUNK):
                y = i * CHUNK + j
                g_next = across(y + 2)
                u_after = g_here + g_next
                q = u_before + u_after
                m = mb[x, y].astype(F32)
                applied = dg[x, pl.ds(y, 1), :] * m - rs[x, pl.ds(y, 1), :] * q
                ab[y] = applied.astype(BF16)
                g_here, u_before = g_next, u_after
            left = along_lanes([mb[x, i * CHUNK + j] for j in range(CHUNK)])
            right = along_lanes([ab[i * CHUNK + j] for j in range(CHUNK)])
            return g_here, u_before, total + row_dot(left, right)

        first = across(1)
        carry = lax.fori_loop(0, c_y // CHUNK, step, (first, first, total))
        return carry[2]

    own_ref[0, 0] = lax.fori_loop(0, c_x, apply_slab, jnp.zeros((rows, rows), F32))

    def half_sum(d):
        from_face(d, 0).wait_recv()
        mine, mine_at, other, depth = [
            (sb.at[0], half_y, rxm, half_y),
            (vx, 0, rxp, half_y),
            (sy0, half_x, rym, half_x),
            (vy, 0, ryp, half_x),
        ][d]
        face_ref[0, 0, :, d * rows : (d + 1) * rows] = block_dot(mine, mine_at, other, 0, depth)
        pout[d, :, 0:rows] = block_dot(other, 0, mine, mine_at, depth)
        to_face(d, 1).start()

    for d in (2, 3, 0, 1):
        guarded(faces[d][0], lambda d=d: half_sum(d))

    for d in range(4):

        def corner_sum(d=d):
            from_corner(d).wait_recv()
            x, y = (0, c_x - 1)[d // 2], (0, c_y - 1)[d % 2]
            mine = (-0.25 * zp[x + 1, y + 1]).astype(BF16)
            corner_ref[0, 0, :, d * rows : (d + 1) * rows] = row_dot(mine, rc[d])

        def corner_zero(d=d):
            corner_ref[0, 0, :, d * rows : (d + 1) * rows] = jnp.zeros((rows, rows), F32)

        guarded(diagonals[d][0], corner_sum)
        guarded(jnp.logical_not(diagonals[d][0]), corner_zero)

    off_ref[...] = jnp.zeros(off_ref.shape, jnp.int32)
    for far in range(1, n_y):

        def earlier(far=far):
            to_peer(far).wait_recv()
            off_ref[...] += cr[far, 0:1, 0:1]

        guarded(iy >= far, earlier)

    def finish(d):
        from_face(d, 1).wait_recv()
        face_ref[0, 0, :, d * rows : (d + 1) * rows] += pin[d, :, 0:rows]

    def face_zero(d):
        face_ref[0, 0, :, d * rows : (d + 1) * rows] = jnp.zeros((rows, rows), F32)

    for d in (2, 3, 0, 1):
        guarded(faces[d][0], lambda d=d: finish(d))
        guarded(jnp.logical_not(faces[d][0]), lambda d=d: face_zero(d))

    def sent(d):
        to_face(d, 0).wait_send()
        to_face(d, 1).wait_send()

    for d in range(4):
        guarded(faces[d][0], lambda d=d: sent(d))
        guarded(diagonals[d][0], lambda d=d: to_corner(d).wait_send())
    for far in range(1, n_y):
        guarded(iy + far < n_y, lambda far=far: to_peer(far).wait_send())


def on_device(n_x, n_y, vectors, root_stiff, diag_coef, counts):
    rows, c_x, c_y, c_z = vectors.shape
    half_x, half_y = c_x // 2, c_y // 2
    vmem = pltpu.VMEM
    return pl.pallas_call(
        functools.partial(kernel, n_x, n_y),
        out_shape=(
            jax.ShapeDtypeStruct((1, 1, rows, rows), F32),
            jax.ShapeDtypeStruct((1, 1, rows, 4 * rows), F32),
            jax.ShapeDtypeStruct((1, 1, rows, 4 * rows), F32),
            jax.ShapeDtypeStruct((1, 1), jnp.int32),
        ),
        in_specs=[
            pl.BlockSpec(memory_space=pl.ANY),
            pl.BlockSpec(memory_space=pl.ANY),
            pl.BlockSpec(memory_space=pl.ANY),
            pl.BlockSpec(memory_space=pltpu.SMEM),
        ],
        out_specs=[pl.BlockSpec(memory_space=vmem)] * 4,
        scratch_shapes=[
            vmem((c_x, rows, c_y, c_z), BF16),
            vmem((c_x, c_y, c_z), F32),
            vmem((c_x, c_y, c_z), F32),
            vmem((rows * c_y, c_z), F32),
            vmem((c_x, c_y, rows, c_z), BF16),
            vmem((c_x, c_y, rows, c_z), BF16),
            vmem((c_x + 2, c_y + 2, rows, c_z), F32),
            vmem((c_y, rows, c_z), BF16),
            vmem((c_y, rows, c_z), BF16),
            vmem((c_x, rows, c_z), BF16),
            vmem((c_x, rows, c_z), BF16),
            vmem((half_y, rows, c_z), BF16),
            vmem((half_y, rows, c_z), BF16),
            vmem((half_x, rows, c_z), BF16),
            vmem((half_x, rows, c_z), BF16),
            vmem((4, rows, c_z), BF16),
            vmem((4, rows, c_z), F32),
            vmem((4, rows, c_z), F32),
            vmem((8, c_z), jnp.int32),
            vmem((n_y, 8, c_z), jnp.int32),
            pltpu.SemaphoreType.DMA((c_x + 2,)),
            pltpu.SemaphoreType.DMA((12,)),
            pltpu.SemaphoreType.DMA((12,)),
            pltpu.SemaphoreType.DMA((n_y,)),
            pltpu.SemaphoreType.DMA((n_y,)),
        ],
        compiler_params=pltpu.CompilerParams(
            collective_id=0, has_side_effects=True, vmem_limit_bytes=60 * 1024 * 1024
        ),
        cost_estimate=pl.CostEstimate(flops=600_000_000, bytes_accessed=5_000_000, transcendentals=0),
    )(vectors, root_stiff, diag_coef, counts)


def solution(mesh):
    n_x, n_y = mesh.shape["sx"], mesh.shape["sy"]
    return jax.shard_map(
        functools.partial(on_device, n_x, n_y),
        mesh=mesh,
        in_specs=(
            P(None, "sx", "sy", None),
            P("sx", "sy", None),
            P("sx", "sy", None),
            P("sx", "sy"),
        ),
        out_specs=(
            P("sx", "sy", None, None),
            P("sx", "sy", None, None),
            P("sx", "sy", None, None),
            P("sx", "sy"),
        ),
        check_vma=False,
    )
```

```python
import functools

import jax
import jax.numpy as jnp
from jax import lax
from jax.experimental import pallas as pl
from jax.experimental.pallas import tpu as pltpu
from jax.sharding import PartitionSpec as P

MESH = pl.DeviceIdType.MESH
F32 = jnp.float32
BF16 = jnp.bfloat16


def row_dot(left, right):
    return lax.dot_general(left, right, (((1,), (1,)), ((), ())), preferred_element_type=F32)


def along_lanes(pieces):
    return jnp.concatenate(pieces, axis=1)


def block_dot(left_ref, left_start, right_ref, right_start, count):
    return row_dot(
        along_lanes([left_ref[left_start + i] for i in range(count)]),
        along_lanes([right_ref[right_start + i] for i in range(count)]),
    )


def kernel(
    n_x,
    n_y,
    vec_ref,
    rs_ref,
    dg_ref,
    cnt_ref,
    own_ref,
    face_ref,
    corner_ref,
    off_ref,
    vv,
    rs,
    dg,
    cnt,
    wide,
    mb,
    sx0,
    sy0,
    sy1,
    zp,
    ab,
    vx,
    vy,
    rxm,
    rxp,
    rym,
    ryp,
    rc,
    pout,
    pin,
    cb,
    cr,
    load_sem,
    send_sem,
    recv_sem,
    csend_sem,
    crecv_sem,
):
    rows, c_x, c_y, c_z = vec_ref.shape
    half_x, half_y = c_x // 2, c_y // 2
    pitch = c_y + 1
    ix, iy = lax.axis_index("sx"), lax.axis_index("sy")

    def load(x):
        return pltpu.make_async_copy(vec_ref.at[:, x], vv.at[x], load_sem.at[x])

    rs_load = pltpu.make_async_copy(rs_ref, rs, load_sem.at[c_x])
    dg_load = pltpu.make_async_copy(dg_ref, dg, load_sem.at[c_x + 1])
    cnt_load = pltpu.make_async_copy(cnt_ref, cnt, load_sem.at[c_x + 2])
    cnt_load.start()
    load(0).start()
    rs_load.start()
    load(c_x - 1).start()
    for x in range(1, c_x - 1):
        load(x).start()
    dg_load.start()

    low_x, high_x = ix > 0, ix < n_x - 1
    low_y, high_y = iy > 0, iy < n_y - 1
    faces = [
        (low_x, (ix - 1, iy)),
        (high_x, (ix + 1, iy)),
        (low_y, (ix, iy - 1)),
        (high_y, (ix, iy + 1)),
    ]
    diagonals = [
        (low_x & low_y, (ix - 1, iy - 1)),
        (low_x & high_y, (ix - 1, iy + 1)),
        (high_x & low_y, (ix + 1, iy - 1)),
        (high_x & high_y, (ix + 1, iy + 1)),
    ]

    barrier = pltpu.get_barrier_semaphore()
    for there, device in faces + diagonals:

        @pl.when(there)
        def _(device=device):
            pl.semaphore_signal(barrier, inc=1, device_id=device, device_id_type=MESH)

    for far in range(2, n_y):

        @pl.when(iy >= far)
        def _(far=far):
            pl.semaphore_signal(barrier, inc=1, device_id=(ix, iy - far), device_id_type=MESH)

    beside = sum(there.astype(jnp.int32) for there, _ in faces + diagonals)
    later = jnp.maximum(n_y - 2 - iy, 0)

    lane_r = lax.broadcasted_iota(jnp.int32, (c_z, c_z), 0)
    lane_c = lax.broadcasted_iota(jnp.int32, (c_z, c_z), 1)
    apart = jnp.abs(lane_r - lane_c)
    smooth = jnp.where(apart == 0, 1.0, jnp.where(apart == 1, 0.5, 0.0)).astype(BF16)

    def zero_row(y, _):
        zp[0, y] = jnp.zeros((rows, c_z), F32)
        zp[c_x + 1, y] = jnp.zeros((rows, c_z), F32)
        return _

    lax.fori_loop(0, c_y + 2, zero_row, 0)
    for x in range(1, c_x + 1):
        zp[x, 0] = jnp.zeros((rows, c_z), F32)
        zp[x, c_y + 1] = jnp.zeros((rows, c_z), F32)

    cnt_load.wait()
    cb[...] = jnp.broadcast_to(cnt[...], cb.shape)
    keep = lax.broadcasted_iota(jnp.int32, (rows, c_z), 0) < cnt[...]

    def scale(x, edge=False):
        load(x).wait()
        for a in range(rows):
            wide[a * pitch : a * pitch + c_y, :] = vv[x, a].astype(F32)
        pieces = []
        for y in range(c_y):
            m = jnp.where(keep, wide[pl.ds(y, rows, stride=pitch), :], 0.0)
            s = (m * rs[x, y : y + 1, :]).astype(BF16)
            mb[x, y] = m.astype(BF16)
            if edge:
                sx0[y] = s
            if y == 0:
                sy0[x] = s
            if y == c_y - 1:
                sy1[x] = s
            pieces.append(s)
        z = jnp.dot(jnp.concatenate(pieces, axis=0), smooth, preferred_element_type=F32)
        for y in range(c_y):
            zp[x + 1, y + 1] = z[y * rows : (y + 1) * rows]

    rs_load.wait()
    scale(0, True)
    scale(c_x - 1)

    for y in range(c_y):
        vx[y] = (-0.25 * ((zp[c_x, y] + zp[c_x, y + 2]) + 2.0 * zp[c_x, y + 1])).astype(BF16)

    pl.semaphore_wait(barrier, beside + later)

    def to_face(d, phase, to=None):
        opposite = d ^ 1
        if phase == 0:
            src, dst = [
                (sx0.at[pl.ds(0, half_y)], rxp),
                (vx.at[pl.ds(half_y, half_y)], rxm),
                (sy0.at[pl.ds(0, half_x)], ryp),
                (vy.at[pl.ds(half_x, half_x)], rym),
            ][d]
        else:
            src, dst = pout.at[d], pin.at[opposite]
        return pltpu.make_async_remote_copy(
            src_ref=src,
            dst_ref=dst,
            send_sem=send_sem.at[phase * 4 + d],
            recv_sem=recv_sem.at[phase * 4 + opposite],
            device_id=faces[d if to is None else to][1],
            device_id_type=MESH,
        )

    def to_corner(d, to=None):
        opposite = 3 - d
        side = (sy0, sy1)[d % 2]
        return pltpu.make_async_remote_copy(
            src_ref=side.at[(0, c_x - 1)[d // 2]],
            dst_ref=rc.at[opposite],
            send_sem=send_sem.at[8 + d],
            recv_sem=recv_sem.at[8 + opposite],
            device_id=diagonals[d if to is None else to][1],
            device_id_type=MESH,
        )

    def from_face(d, phase):
        return to_face(d ^ 1, phase, d)

    def from_corner(d):
        return to_corner(3 - d, d)

    def to_peer(far):
        return pltpu.make_async_remote_copy(
            src_ref=cb,
            dst_ref=cr.at[far],
            send_sem=csend_sem.at[far],
            recv_sem=crecv_sem.at[far],
            device_id=(ix, iy + far),
            device_id_type=MESH,
        )

    def guarded(there, action):
        @pl.when(there)
        def _():
            action()

    for d in (1, 0):
        guarded(faces[d][0], lambda d=d: to_face(d, 0).start())
    for d in range(4):
        guarded(diagonals[d][0], lambda d=d: to_corner(d).start())
    for far in range(1, n_y):
        guarded(iy + far < n_y, lambda far=far: to_peer(far).start())

    def scale_step(x, _):
        scale(x)
        return _

    lax.fori_loop(1, c_x - 1, scale_step, 0)

    for x in range(c_x):
        vy[x] = (-0.25 * ((zp[x, c_y] + zp[x + 2, c_y]) + 2.0 * zp[x + 1, c_y])).astype(BF16)
    for d in (3, 2):
        guarded(faces[d][0], lambda d=d: to_face(d, 0).start())

    dg_load.wait()
    dg[...] = dg[...] + rs[...] * rs[...]
    rs[...] = rs[...] * 0.25

    def apply(x, slot):
        def across(y):
            near = zp[x + 1, y]
            return (zp[x, y] + near) + (near + zp[x + 2, y])

        here = across(1)
        before = here
        for y in range(c_y):
            ahead = across(y + 2)
            after = here + ahead
            m = mb[x, y].astype(F32)
            applied = dg[x, pl.ds(y, 1), :] * m - rs[x, pl.ds(y, 1), :] * (before + after)
            ab[slot, y] = applied.astype(BF16)
            here, before = ahead, after

    def product(x, slot):
        return block_dot(mb.at[x], 0, ab.at[slot], 0, c_y)

    apply(0, 0)

    def own_step(i, total):
        x = 2 * i
        total = total + product(x, 0)
        apply(x + 1, 1)
        total = total + product(x + 1, 1)
        apply(x + 2, 0)
        return total

    total = lax.fori_loop(0, c_x // 2 - 1, own_step, jnp.zeros((rows, rows), F32))
    total = total + product(c_x - 2, 0)
    apply(c_x - 1, 1)
    own_ref[0, 0] = total + product(c_x - 1, 1)

    def half_sum(d):
        from_face(d, 0).wait_recv()
        mine, mine_at, other, depth = [
            (sx0, half_y, rxm, half_y),
            (vx, 0, rxp, half_y),
            (sy0, half_x, rym, half_x),
            (vy, 0, ryp, half_x),
        ][d]
        pout[d, :, 0:rows] = block_dot(other, 0, mine, mine_at, depth)
        to_face(d, 1).start()
        face_ref[0, 0, :, d * rows : (d + 1) * rows] = block_dot(mine, mine_at, other, 0, depth)

    for d in (2, 3, 0, 1):
        guarded(faces[d][0], lambda d=d: half_sum(d))

    for d in range(4):

        def corner_sum(d=d):
            from_corner(d).wait_recv()
            x, y = (0, c_x - 1)[d // 2], (0, c_y - 1)[d % 2]
            mine = (-0.25 * zp[x + 1, y + 1]).astype(BF16)
            corner_ref[0, 0, :, d * rows : (d + 1) * rows] = row_dot(mine, rc[d])

        def corner_zero(d=d):
            corner_ref[0, 0, :, d * rows : (d + 1) * rows] = jnp.zeros((rows, rows), F32)

        guarded(diagonals[d][0], corner_sum)
        guarded(jnp.logical_not(diagonals[d][0]), corner_zero)

    off_ref[...] = jnp.zeros(off_ref.shape, jnp.int32)
    for far in range(1, n_y):

        def earlier(far=far):
            to_peer(far).wait_recv()
            off_ref[...] += cr[far, 0:1, 0:1]

        guarded(iy >= far, earlier)

    def finish(d):
        from_face(d, 1).wait_recv()
        face_ref[0, 0, :, d * rows : (d + 1) * rows] += pin[d, :, 0:rows]

    def face_zero(d):
        face_ref[0, 0, :, d * rows : (d + 1) * rows] = jnp.zeros((rows, rows), F32)

    for d in (2, 3, 0, 1):
        guarded(faces[d][0], lambda d=d: finish(d))
        guarded(jnp.logical_not(faces[d][0]), lambda d=d: face_zero(d))

    def sent(d):
        to_face(d, 0).wait_send()
        to_face(d, 1).wait_send()

    for d in range(4):
        guarded(faces[d][0], lambda d=d: sent(d))
        guarded(diagonals[d][0], lambda d=d: to_corner(d).wait_send())
    for far in range(1, n_y):
        guarded(iy + far < n_y, lambda far=far: to_peer(far).wait_send())


def hand_on(*refs):
    n = (len(refs) - 1) // 2
    copies = [pltpu.make_async_copy(refs[i], refs[n + i], refs[-1].at[i]) for i in range(n)]
    for copy in copies:
        copy.start()
    for copy in copies:
        copy.wait()


def on_device(n_x, n_y, vectors, root_stiff, diag_coef, counts):
    rows, c_x, c_y, c_z = vectors.shape
    half_x, half_y = c_x // 2, c_y // 2
    vmem = pltpu.VMEM
    results = (
        jax.ShapeDtypeStruct((1, 1, rows, rows), F32),
        jax.ShapeDtypeStruct((1, 1, rows, 4 * rows), F32),
        jax.ShapeDtypeStruct((1, 1, rows, 4 * rows), F32),
        jax.ShapeDtypeStruct((1, 1), jnp.int32),
    )
    anywhere = pl.BlockSpec(memory_space=pl.ANY)
    outputs = pl.pallas_call(
        functools.partial(kernel, n_x, n_y),
        out_shape=results,
        in_specs=[anywhere] * 3 + [pl.BlockSpec(memory_space=pltpu.HBM)],
        out_specs=[pl.BlockSpec(memory_space=vmem)] * 4,
        scratch_shapes=[
            vmem((c_x, rows, c_y, c_z), BF16),
            vmem((c_x, c_y, c_z), F32),
            vmem((c_x, c_y, c_z), F32),
            vmem((1, 1), jnp.int32),
            vmem((rows * (c_y + 1) + 7, c_z), F32),
            vmem((c_x, c_y, rows, c_z), BF16),
            vmem((c_y, rows, c_z), BF16),
            vmem((c_x, rows, c_z), BF16),
            vmem((c_x, rows, c_z), BF16),
            vmem((c_x + 2, c_y + 2, rows, c_z), F32),
            vmem((2, c_y, rows, c_z), BF16),
            vmem((c_y, rows, c_z), BF16),
            vmem((c_x, rows, c_z), BF16),
            vmem((half_y, rows, c_z), BF16),
            vmem((half_y, rows, c_z), BF16),
            vmem((half_x, rows, c_z), BF16),
            vmem((half_x, rows, c_z), BF16),
            vmem((4, rows, c_z), BF16),
            vmem((4, rows, c_z), F32),
            vmem((4, rows, c_z), F32),
            vmem((8, c_z), jnp.int32),
            vmem((n_y, 8, c_z), jnp.int32),
            pltpu.SemaphoreType.DMA((c_x + 3,)),
            pltpu.SemaphoreType.DMA((12,)),
            pltpu.SemaphoreType.DMA((12,)),
            pltpu.SemaphoreType.DMA((n_y,)),
            pltpu.SemaphoreType.DMA((n_y,)),
        ],
        compiler_params=pltpu.CompilerParams(
            collective_id=0, has_side_effects=True, vmem_limit_bytes=60 * 1024 * 1024
        ),
        cost_estimate=pl.CostEstimate(flops=600_000_000, bytes_accessed=5_000_000, transcendentals=0),
        name="coarse",
    )(vectors, root_stiff, diag_coef, counts)
    return pl.pallas_call(
        hand_on,
        out_shape=results,
        in_specs=[anywhere] * len(results),
        out_specs=[anywhere] * len(results),
        scratch_shapes=[pltpu.SemaphoreType.DMA((len(results),))],
        name="results",
    )(*outputs)


def solution(mesh):
    n_x, n_y = mesh.shape["sx"], mesh.shape["sy"]
    return jax.shard_map(
        functools.partial(on_device, n_x, n_y),
        mesh=mesh,
        in_specs=(
            P(None, "sx", "sy", None),
            P("sx", "sy", None),
            P("sx", "sy", None),
            P("sx", "sy"),
        ),
        out_specs=(
            P("sx", "sy", None, None),
            P("sx", "sy", None, None),
            P("sx", "sy", None, None),
            P("sx", "sy"),
        ),
        check_vma=False,
    )
```

```python
import functools

import jax
import jax.numpy as jnp
from jax import lax
from jax.experimental import pallas as pl
from jax.experimental.pallas import tpu as pltpu
from jax.sharding import PartitionSpec as P

MESH = pl.DeviceIdType.MESH
F32 = jnp.float32
BF16 = jnp.bfloat16


def row_dot(left, right):
    return lax.dot_general(left, right, (((1,), (1,)), ((), ())), preferred_element_type=F32)


def along_lanes(pieces):
    return jnp.concatenate(pieces, axis=1)


def block_dot(left_ref, left_start, right_ref, right_start, count):
    return row_dot(
        along_lanes([left_ref[left_start + i] for i in range(count)]),
        along_lanes([right_ref[right_start + i] for i in range(count)]),
    )


def kernel(
    n_x,
    n_y,
    vec_ref,
    rs_ref,
    dg_ref,
    cnt_ref,
    own_ref,
    face_ref,
    corner_ref,
    off_ref,
    vv,
    rs,
    dg,
    cnt,
    wide,
    mb,
    sx,
    sy0,
    sy1,
    lean,
    zp,
    ab,
    vx,
    vy,
    rx,
    ry,
    rc,
    pout,
    pin,
    cb,
    cr,
    load_sem,
    send_sem,
    recv_sem,
    csend_sem,
    crecv_sem,
):
    rows, c_x, c_y, c_z = vec_ref.shape
    half_x = c_x // 2
    pitch = c_y + 1
    ix, iy = lax.axis_index("sx"), lax.axis_index("sy")

    def load(x):
        return pltpu.make_async_copy(vec_ref.at[:, x], vv.at[x], load_sem.at[x])

    rs_load = pltpu.make_async_copy(rs_ref, rs, load_sem.at[c_x])
    dg_load = pltpu.make_async_copy(dg_ref, dg, load_sem.at[c_x + 1])
    cnt_load = pltpu.make_async_copy(cnt_ref, cnt, load_sem.at[c_x + 2])
    cnt_load.start()
    load(0).start()
    rs_load.start()
    load(c_x - 1).start()
    for x in range(1, c_x - 1):
        load(x).start()
    dg_load.start()

    low_x, high_x = ix > 0, ix < n_x - 1
    low_y, high_y = iy > 0, iy < n_y - 1
    faces = [
        (low_x, (ix - 1, iy)),
        (high_x, (ix + 1, iy)),
        (low_y, (ix, iy - 1)),
        (high_y, (ix, iy + 1)),
    ]
    diagonals = [
        (low_x & low_y, (ix - 1, iy - 1)),
        (low_x & high_y, (ix - 1, iy + 1)),
        (high_x & low_y, (ix + 1, iy - 1)),
        (high_x & high_y, (ix + 1, iy + 1)),
    ]

    barrier = pltpu.get_barrier_semaphore()
    for there, device in faces + diagonals:

        @pl.when(there)
        def _(device=device):
            pl.semaphore_signal(barrier, inc=1, device_id=device, device_id_type=MESH)

    for far in range(2, n_y):

        @pl.when(iy >= far)
        def _(far=far):
            pl.semaphore_signal(barrier, inc=1, device_id=(ix, iy - far), device_id_type=MESH)

    beside = sum(there.astype(jnp.int32) for there, _ in faces + diagonals)
    later = jnp.maximum(n_y - 2 - iy, 0)

    lane_r = lax.broadcasted_iota(jnp.int32, (c_z, c_z), 0)
    lane_c = lax.broadcasted_iota(jnp.int32, (c_z, c_z), 1)
    apart = jnp.abs(lane_r - lane_c)
    smooth = jnp.where(apart == 0, 1.0, jnp.where(apart == 1, 0.5, 0.0)).astype(BF16)

    def zero_row(y, _):
        zp[0, y] = jnp.zeros((rows, c_z), F32)
        zp[c_x + 1, y] = jnp.zeros((rows, c_z), F32)
        return _

    lax.fori_loop(0, c_y + 2, zero_row, 0)
    for x in range(1, c_x + 1):
        zp[x, 0] = jnp.zeros((rows, c_z), F32)
        zp[x, c_y + 1] = jnp.zeros((rows, c_z), F32)

    cnt_load.wait()
    cb[...] = jnp.broadcast_to(cnt[...], cb.shape)
    keep = lax.broadcasted_iota(jnp.int32, (rows, c_z), 0) < cnt[...]

    def widen(x):
        load(x).wait()
        for a in range(rows):
            wide[x, a * pitch : a * pitch + c_y, :] = vv[x, a].astype(F32)

    def row(x, y):
        m = jnp.where(keep, wide[x, pl.ds(y, rows, stride=pitch), :], 0.0)
        return m, m * rs[x, y : y + 1, :]

    def scale(x, side=None):
        pieces = []
        for y in range(c_y):
            m, s = row(x, y)
            s = s.astype(BF16)
            mb[x, y] = m.astype(BF16)
            if side is not None:
                sx[side, y] = s
            pieces.append(s)
        z = jnp.dot(jnp.concatenate(pieces, axis=0), smooth, preferred_element_type=F32)
        for y in range(c_y):
            zp[x + 1, y + 1] = z[y * rows : (y + 1) * rows]

    rs_load.wait()
    widen(0)
    scale(0, 0)
    widen(c_x - 1)
    scale(c_x - 1, 1)

    def widen_step(x, _):
        widen(x)
        return _

    lax.fori_loop(1, c_x - 1, widen_step, 0)
    ends = []
    for x in range(c_x):
        sy0[x] = row(x, 0)[1].astype(BF16)
        s = row(x, c_y - 1)[1]
        sy1[x] = s.astype(BF16)
        ends.append(s)
    ends.append(jnp.zeros((rows, c_z), F32))
    for x in range(half_x, c_x):
        lean[x - half_x] = (ends[x] + 0.5 * (ends[x - 1] + ends[x + 1])).astype(BF16)

    pl.semaphore_wait(barrier, beside + later)

    def to_face(d, phase, to=None):
        opposite = d ^ 1
        if phase == 0:
            src, dst = [
                (sx.at[0], rx.at[1]),
                (sx.at[1], rx.at[0]),
                (sy0.at[pl.ds(0, half_x)], ry.at[1]),
                (lean, ry.at[0]),
            ][d]
        else:
            src, dst = pout.at[d - 2], pin.at[opposite - 2]
        return pltpu.make_async_remote_copy(
            src_ref=src,
            dst_ref=dst,
            send_sem=send_sem.at[phase * 4 + d],
            recv_sem=recv_sem.at[phase * 4 + opposite],
            device_id=faces[d if to is None else to][1],
            device_id_type=MESH,
        )

    def to_corner(d, to=None):
        opposite = 3 - d
        side = (sy0, sy1)[d % 2]
        return pltpu.make_async_remote_copy(
            src_ref=side.at[(0, c_x - 1)[d // 2]],
            dst_ref=rc.at[opposite],
            send_sem=send_sem.at[8 + d],
            recv_sem=recv_sem.at[8 + opposite],
            device_id=diagonals[d if to is None else to][1],
            device_id_type=MESH,
        )

    def from_face(d, phase):
        return to_face(d ^ 1, phase, d)

    def from_corner(d):
        return to_corner(3 - d, d)

    def to_peer(far):
        return pltpu.make_async_remote_copy(
            src_ref=cb,
            dst_ref=cr.at[far],
            send_sem=csend_sem.at[far],
            recv_sem=crecv_sem.at[far],
            device_id=(ix, iy + far),
            device_id_type=MESH,
        )

    def guarded(there, action):
        @pl.when(there)
        def _():
            action()

    for d in (3, 2, 1, 0):
        guarded(faces[d][0], lambda d=d: to_face(d, 0).start())
    for d in range(4):
        guarded(diagonals[d][0], lambda d=d: to_corner(d).start())
    for far in range(1, n_y):
        guarded(iy + far < n_y, lambda far=far: to_peer(far).start())

    def scale_step(x, _):
        scale(x)
        return _

    lax.fori_loop(1, c_x - 1, scale_step, 0)

    for side, x in enumerate((1, c_x)):
        for y in range(c_y):
            vx[side, y] = (
                -0.25 * ((zp[x, y] + zp[x, y + 2]) + 2.0 * zp[x, y + 1])
            ).astype(BF16)
    for x in range(half_x):
        vy[0, x] = (-0.5 * zp[half_x + x + 1, 1]).astype(BF16)
        vy[1, x] = (
            -0.25 * ((zp[x, c_y] + zp[x + 2, c_y]) + 2.0 * zp[x + 1, c_y])
        ).astype(BF16)

    dg_load.wait()
    dg[...] = dg[...] + rs[...] * rs[...]
    rs[...] = rs[...] * 0.25

    def apply(x, slot):
        def across(y):
            near = zp[x + 1, y]
            return (zp[x, y] + near) + (near + zp[x + 2, y])

        here = across(1)
        before = here
        for y in range(c_y):
            ahead = across(y + 2)
            after = here + ahead
            m = mb[x, y].astype(F32)
            applied = dg[x, pl.ds(y, 1), :] * m - rs[x, pl.ds(y, 1), :] * (before + after)
            ab[slot, y] = applied.astype(BF16)
            here, before = ahead, after

    def product(x, slot):
        return block_dot(mb.at[x], 0, ab.at[slot], 0, c_y)

    apply(0, 0)

    def own_step(i, total):
        x = 2 * i
        total = total + product(x, 0)
        apply(x + 1, 1)
        total = total + product(x + 1, 1)
        apply(x + 2, 0)
        return total

    def half_sum(d):
        from_face(d, 0).wait_recv()
        mine, other = vy.at[d - 2], ry.at[d - 2]
        pout[d - 2, :, 0:rows] = block_dot(other, 0, mine, 0, half_x)
        to_face(d, 1).start()
        face_ref[0, 0, :, d * rows : (d + 1) * rows] = block_dot(mine, 0, other, 0, half_x)

    steps = c_x // 2 - 1
    total = lax.fori_loop(0, steps - 1, own_step, jnp.zeros((rows, rows), F32))
    for d in (2, 3):
        guarded(faces[d][0], lambda d=d: half_sum(d))
    total = lax.fori_loop(steps - 1, steps, own_step, total)
    total = total + product(c_x - 2, 0)
    apply(c_x - 1, 1)
    own_ref[0, 0] = total + product(c_x - 1, 1)

    for d in range(4):

        def corner_sum(d=d):
            from_corner(d).wait_recv()
            x, y = (0, c_x - 1)[d // 2], (0, c_y - 1)[d % 2]
            mine = (-0.25 * zp[x + 1, y + 1]).astype(BF16)
            corner_ref[0, 0, :, d * rows : (d + 1) * rows] = row_dot(mine, rc[d])

        def corner_zero(d=d):
            corner_ref[0, 0, :, d * rows : (d + 1) * rows] = jnp.zeros((rows, rows), F32)

        guarded(diagonals[d][0], corner_sum)
        guarded(jnp.logical_not(diagonals[d][0]), corner_zero)

    off_ref[...] = jnp.zeros(off_ref.shape, jnp.int32)
    for far in range(1, n_y):

        def earlier(far=far):
            to_peer(far).wait_recv()
            off_ref[...] += cr[far, 0:1, 0:1]

        guarded(iy >= far, earlier)

    def finish_y(d):
        from_face(d, 1).wait_recv()
        face_ref[0, 0, :, d * rows : (d + 1) * rows] += pin[d - 2, :, 0:rows]

    def finish_x(d):
        from_face(d, 0).wait_recv()
        face_ref[0, 0, :, d * rows : (d + 1) * rows] = block_dot(vx.at[d], 0, rx.at[d], 0, c_y)

    def face_zero(d):
        face_ref[0, 0, :, d * rows : (d + 1) * rows] = jnp.zeros((rows, rows), F32)

    for d in (2, 3, 0, 1):
        guarded(faces[d][0], lambda d=d: (finish_x if d < 2 else finish_y)(d))
        guarded(jnp.logical_not(faces[d][0]), lambda d=d: face_zero(d))

    def sent(d):
        to_face(d, 0).wait_send()
        if d >= 2:
            to_face(d, 1).wait_send()

    for d in range(4):
        guarded(faces[d][0], lambda d=d: sent(d))
        guarded(diagonals[d][0], lambda d=d: to_corner(d).wait_send())
    for far in range(1, n_y):
        guarded(iy + far < n_y, lambda far=far: to_peer(far).wait_send())


def hand_on(*refs):
    n = len(refs) // 2
    for i in range(n):
        refs[n + i][...] = refs[i][...]


def on_device(n_x, n_y, vectors, root_stiff, diag_coef, counts):
    rows, c_x, c_y, c_z = vectors.shape
    half_x = c_x // 2
    vmem = pltpu.VMEM
    results = (
        jax.ShapeDtypeStruct((1, 1, rows, rows), F32),
        jax.ShapeDtypeStruct((1, 1, rows, 4 * rows), F32),
        jax.ShapeDtypeStruct((1, 1, rows, 4 * rows), F32),
        jax.ShapeDtypeStruct((1, 1), jnp.int32),
    )
    anywhere = pl.BlockSpec(memory_space=pl.ANY)
    outputs = pl.pallas_call(
        functools.partial(kernel, n_x, n_y),
        out_shape=results,
        in_specs=[anywhere] * 3 + [pl.BlockSpec(memory_space=pltpu.HBM)],
        out_specs=[pl.BlockSpec(memory_space=vmem)] * 4,
        scratch_shapes=[
            vmem((c_x, rows, c_y, c_z), BF16),
            vmem((c_x, c_y, c_z), F32),
            vmem((c_x, c_y, c_z), F32),
            vmem((1, 1), jnp.int32),
            vmem((c_x, rows * (c_y + 1) + 7, c_z), F32),
            vmem((c_x, c_y, rows, c_z), BF16),
            vmem((2, c_y, rows, c_z), BF16),
            vmem((c_x, rows, c_z), BF16),
            vmem((c_x, rows, c_z), BF16),
            vmem((half_x, rows, c_z), BF16),
            vmem((c_x + 2, c_y + 2, rows, c_z), F32),
            vmem((2, c_y, rows, c_z), BF16),
            vmem((2, c_y, rows, c_z), BF16),
            vmem((2, half_x, rows, c_z), BF16),
            vmem((2, c_y, rows, c_z), BF16),
            vmem((2, half_x, rows, c_z), BF16),
            vmem((4, rows, c_z), BF16),
            vmem((2, rows, c_z), F32),
            vmem((2, rows, c_z), F32),
            vmem((8, c_z), jnp.int32),
            vmem((n_y, 8, c_z), jnp.int32),
            pltpu.SemaphoreType.DMA((c_x + 3,)),
            pltpu.SemaphoreType.DMA((12,)),
            pltpu.SemaphoreType.DMA((12,)),
            pltpu.SemaphoreType.DMA((n_y,)),
            pltpu.SemaphoreType.DMA((n_y,)),
        ],
        compiler_params=pltpu.CompilerParams(
            collective_id=0, has_side_effects=True, vmem_limit_bytes=60 * 1024 * 1024
        ),
        cost_estimate=pl.CostEstimate(flops=600_000_000, bytes_accessed=5_000_000, transcendentals=0),
        name="coarse",
    )(vectors, root_stiff, diag_coef, counts)
    return pl.pallas_call(
        hand_on,
        out_shape=results,
        in_specs=[pl.BlockSpec(memory_space=vmem)] * len(results),
        out_specs=[pl.BlockSpec(memory_space=vmem)] * len(results),
        name="results",
    )(*outputs)


def solution(mesh):
    n_x, n_y = mesh.shape["sx"], mesh.shape["sy"]
    return jax.shard_map(
        functools.partial(on_device, n_x, n_y),
        mesh=mesh,
        in_specs=(
            P(None, "sx", "sy", None),
            P("sx", "sy", None),
            P("sx", "sy", None),
            P("sx", "sy"),
        ),
        out_specs=(
            P("sx", "sy", None, None),
            P("sx", "sy", None, None),
            P("sx", "sy", None, None),
            P("sx", "sy"),
        ),
        check_vma=False,
    )
```

```python
import functools

import jax
import jax.numpy as jnp
from jax import lax
from jax.experimental import pallas as pl
from jax.experimental.pallas import tpu as pltpu
from jax.sharding import PartitionSpec as P

MESH = pl.DeviceIdType.MESH
F32 = jnp.float32
BF16 = jnp.bfloat16


def row_dot(left, right):
    return lax.dot_general(left, right, (((1,), (1,)), ((), ())), preferred_element_type=F32)


def along_lanes(pieces):
    return jnp.concatenate(pieces, axis=1)


def block_dot(left_ref, left_start, right_ref, right_start, count):
    return row_dot(
        along_lanes([left_ref[left_start + i] for i in range(count)]),
        along_lanes([right_ref[right_start + i] for i in range(count)]),
    )


def kernel(
    n_x,
    n_y,
    vec_ref,
    rs_ref,
    dg_ref,
    cnt_ref,
    own_ref,
    face_ref,
    corner_ref,
    off_ref,
    vv,
    rs,
    dg,
    cnt,
    wide,
    mb,
    sx,
    sy0,
    sy1,
    zp,
    ab,
    vx,
    vy,
    rx,
    ry,
    rc,
    rr,
    cb,
    cb_last,
    cr,
    load_sem,
    send_sem,
    recv_sem,
    csend_sem,
    crecv_sem,
    relay_sem,
):
    rows, c_x, c_y, c_z = vec_ref.shape
    rounds = cb.shape[0]
    pitch = c_y + 1
    ix, iy = lax.axis_index("sx"), lax.axis_index("sy")

    def load(x):
        return pltpu.make_async_copy(vec_ref.at[:, x], vv.at[x], load_sem.at[x])

    rs_load = pltpu.make_async_copy(rs_ref, rs, load_sem.at[c_x])
    dg_load = pltpu.make_async_copy(dg_ref, dg, load_sem.at[c_x + 1])
    cnt_load = pltpu.make_async_copy(cnt_ref, cnt, load_sem.at[c_x + 2])
    cnt_load.start()
    load(0).start()
    rs_load.start()
    load(c_x - 1).start()
    for x in range(1, c_x - 1):
        load(x).start()
    dg_load.start()

    low_x, high_x = ix > 0, ix < n_x - 1
    low_y, high_y = iy > 0, iy < n_y - 1
    faces = [
        (low_x, (ix - 1, iy)),
        (high_x, (ix + 1, iy)),
        (low_y, (ix, iy - 1)),
        (high_y, (ix, iy + 1)),
    ]
    diagonals = [
        (low_x & low_y, (ix - 1, iy - 1)),
        (low_x & high_y, (ix - 1, iy + 1)),
        (high_x & low_y, (ix + 1, iy - 1)),
        (high_x & high_y, (ix + 1, iy + 1)),
    ]

    barrier = pltpu.get_barrier_semaphore()
    for there, device in faces + diagonals:

        @pl.when(there)
        def _(device=device):
            pl.semaphore_signal(barrier, inc=1, device_id=device, device_id_type=MESH)

    across_low, across_high = n_x // 2 - 1, n_x // 2
    is_origin = (ix == across_low) | (ix == across_high)
    is_relay = (ix == 0) | (ix == n_x - 1)
    via_y = iy + 1 - 2 * lax.rem(iy, 2)
    origin_to = (jnp.where(ix == across_low, n_x - 1, 0), via_y)
    relay_to = (jnp.where(ix == 0, across_low, across_high), via_y)
    relay_from = (jnp.where(ix == 0, across_high, across_low), via_y)
    target_from = (jnp.where(ix == across_low, 0, n_x - 1), via_y)

    @pl.when(is_relay)
    def _():
        pl.semaphore_signal(barrier, inc=1, device_id=relay_from, device_id_type=MESH)

    @pl.when(is_origin)
    def _():
        pl.semaphore_signal(barrier, inc=1, device_id=target_from, device_id_type=MESH)

    greeted = sum(there.astype(jnp.int32) for there, _ in faces + diagonals)
    greeted = greeted + (is_relay | is_origin).astype(jnp.int32)

    lane_r = lax.broadcasted_iota(jnp.int32, (c_z, c_z), 0)
    lane_c = lax.broadcasted_iota(jnp.int32, (c_z, c_z), 1)
    apart = jnp.abs(lane_r - lane_c)
    smooth = jnp.where(apart == 0, 1.0, jnp.where(apart == 1, 0.5, 0.0)).astype(BF16)

    def zero_row(y, _):
        zp[0, y] = jnp.zeros((rows, c_z), F32)
        zp[c_x + 1, y] = jnp.zeros((rows, c_z), F32)
        return _

    lax.fori_loop(0, c_y + 2, zero_row, 0)
    for x in range(1, c_x + 1):
        zp[x, 0] = jnp.zeros((rows, c_z), F32)
        zp[x, c_y + 1] = jnp.zeros((rows, c_z), F32)

    cnt_load.wait()
    cb[0] = jnp.broadcast_to(cnt[...], cb.shape[1:])
    keep = lax.broadcasted_iota(jnp.int32, (rows, c_z), 0) < cnt[...]

    def widen(x):
        load(x).wait()
        for a in range(rows):
            wide[x, a * pitch : a * pitch + c_y, :] = vv[x, a].astype(F32)

    def row(x, y):
        m = jnp.where(keep, wide[x, pl.ds(y, rows, stride=pitch), :], 0.0)
        return m, m * rs[x, y : y + 1, :]

    def scale(x, side=None):
        pieces = []
        for y in range(c_y):
            m, s = row(x, y)
            s = s.astype(BF16)
            mb[x, y] = m.astype(BF16)
            if side is not None:
                sx[side, y] = s
            pieces.append(s)
        z = jnp.dot(jnp.concatenate(pieces, axis=0), smooth, preferred_element_type=F32)
        for y in range(c_y):
            zp[x + 1, y + 1] = z[y * rows : (y + 1) * rows]

    rs_load.wait()
    widen(0)
    scale(0, 0)
    widen(c_x - 1)
    scale(c_x - 1, 1)

    def widen_step(x, _):
        widen(x)
        return _

    lax.fori_loop(1, c_x - 1, widen_step, 0)
    for x in range(c_x):
        sy0[x] = row(x, 0)[1].astype(BF16)
        sy1[x] = row(x, c_y - 1)[1].astype(BF16)

    pl.semaphore_wait(barrier, greeted)

    def to_face(d, part, to=None):
        opposite = d ^ 1
        if d < 2:
            piece = pl.ds(part * (c_y // 2), c_y // 2)
            src, dst = sx.at[d, piece], rx.at[opposite, piece]
        else:
            src, dst = (sy0, sy1)[d - 2], ry.at[opposite - 2]
        return pltpu.make_async_remote_copy(
            src_ref=src,
            dst_ref=dst,
            send_sem=send_sem.at[part * 2 + d if d < 2 else 2 + d],
            recv_sem=recv_sem.at[part * 2 + opposite if d < 2 else 2 + opposite],
            device_id=faces[d if to is None else to][1],
            device_id_type=MESH,
        )

    def from_face(d, part):
        return to_face(d ^ 1, part, d)

    def by_relay(d, leg, chunk):
        opposite = d ^ 1
        piece = pl.ds(c_y // 2 + chunk * (c_y // 4), c_y // 4)
        src, dst = [
            (sx.at[d, piece], rr.at[chunk]),
            (rr.at[chunk], rx.at[opposite, piece]),
        ][leg]
        return pltpu.make_async_remote_copy(
            src_ref=src,
            dst_ref=dst,
            send_sem=relay_sem.at[0, leg, chunk],
            recv_sem=relay_sem.at[1, leg, chunk],
            device_id=(origin_to, relay_to)[leg],
            device_id_type=MESH,
        )

    def to_corner(d, to=None):
        opposite = 3 - d
        side = (sy0, sy1)[d % 2]
        return pltpu.make_async_remote_copy(
            src_ref=side.at[(0, c_x - 1)[d // 2]],
            dst_ref=rc.at[opposite],
            send_sem=send_sem.at[8 + d],
            recv_sem=recv_sem.at[8 + opposite],
            device_id=diagonals[d if to is None else to][1],
            device_id_type=MESH,
        )

    def from_corner(d):
        return to_corner(3 - d, d)

    def to_peer(r, up):
        far = 2**r
        return pltpu.make_async_remote_copy(
            src_ref=cb.at[r],
            dst_ref=cr.at[r, up],
            send_sem=csend_sem.at[r, up],
            recv_sem=crecv_sem.at[r, up],
            device_id=(ix, iy + far if up else iy - far),
            device_id_type=MESH,
        )

    def guarded(there, action):
        @pl.when(there)
        def _():
            action()

    def origin_of(d):
        return ix == (across_high, across_low)[d]

    def send_x(d):
        @pl.when(origin_of(d))
        def _():
            for chunk in range(2):
                by_relay(d, 0, chunk).start()

        @pl.when(jnp.logical_not(origin_of(d)))
        def _():
            to_face(d, 1).start()

        to_face(d, 0).start()

    def send_counts(r):
        guarded(iy + 2**r < n_y, lambda: to_peer(r, 1).start())
        if r + 1 < rounds:
            guarded(iy >= 2**r, lambda: to_peer(r, 0).start())

    def add_counts(r):
        far = 2**r
        cb_next = cb.at[r + 1] if r + 1 < rounds else cb_last
        cb_next[...] = cb[r]

        @pl.when(iy >= far)
        def _():
            to_peer(r, 1).wait_recv()
            cb_next[...] += cr[r, 1]

        if r + 1 < rounds:
            guarded(iy + far < n_y, lambda: to_peer(r, 0).wait_recv())

    send_counts(0)
    for d in (1, 0):
        guarded(faces[d][0], lambda d=d: send_x(d))
    for d in (3, 2):
        guarded(faces[d][0], lambda d=d: to_face(d, 0).start())
    for d in range(4):
        guarded(diagonals[d][0], lambda d=d: to_corner(d).start())

    def scale_step(x, _):
        scale(x)
        return _

    lax.fori_loop(1, c_x - 1, scale_step, 0)

    for side, x in enumerate((1, c_x)):
        for y in range(c_y):
            vx[side, y] = (
                -0.25 * ((zp[x, y] + zp[x, y + 2]) + 2.0 * zp[x, y + 1])
            ).astype(BF16)
    for side, y in enumerate((1, c_y)):
        for x in range(c_x):
            vy[side, x] = (
                -0.25 * ((zp[x, y] + zp[x + 2, y]) + 2.0 * zp[x + 1, y])
            ).astype(BF16)

    dg_load.wait()
    dg[...] = dg[...] + rs[...] * rs[...]
    rs[...] = rs[...] * 0.25

    def apply(x, slot):
        def across(y):
            near = zp[x + 1, y]
            return (zp[x, y] + near) + (near + zp[x + 2, y])

        here = across(1)
        before = here
        for y in range(c_y):
            ahead = across(y + 2)
            after = here + ahead
            m = mb[x, y].astype(F32)
            applied = dg[x, pl.ds(y, 1), :] * m - rs[x, pl.ds(y, 1), :] * (before + after)
            ab[slot, y] = applied.astype(BF16)
            here, before = ahead, after

    def product(x, slot):
        return block_dot(mb.at[x], 0, ab.at[slot], 0, c_y)

    apply(0, 0)

    def own_step(i, total):
        x = 2 * i
        total = total + product(x, 0)
        apply(x + 1, 1)
        total = total + product(x + 1, 1)
        apply(x + 2, 0)
        return total

    def hand_over(d, chunk):
        by_relay(d, 0, chunk).wait_recv()
        by_relay(d, 1, chunk).start()

    total = jnp.zeros((rows, rows), F32)
    for step in range(c_x // 2 - 1):
        if step < rounds - 1:
            add_counts(step)
            send_counts(step + 1)
        total = lax.fori_loop(step, step + 1, own_step, total)
        if step < 2:
            guarded(ix == 0, lambda step=step: hand_over(0, step))
            guarded(ix == n_x - 1, lambda step=step: hand_over(1, step))
    total = total + product(c_x - 2, 0)
    apply(c_x - 1, 1)
    own_ref[0, 0] = total + product(c_x - 1, 1)

    for d in range(4):

        def corner_sum(d=d):
            from_corner(d).wait_recv()
            x, y = (0, c_x - 1)[d // 2], (0, c_y - 1)[d % 2]
            mine = (-0.25 * zp[x + 1, y + 1]).astype(BF16)
            corner_ref[0, 0, :, d * rows : (d + 1) * rows] = row_dot(mine, rc[d])

        def corner_zero(d=d):
            corner_ref[0, 0, :, d * rows : (d + 1) * rows] = jnp.zeros((rows, rows), F32)

        guarded(diagonals[d][0], corner_sum)
        guarded(jnp.logical_not(diagonals[d][0]), corner_zero)

    for r in range(min(c_x // 2 - 1, rounds - 1), rounds):
        add_counts(r)
        if r + 1 < rounds:
            send_counts(r + 1)
    off_ref[...] = cb_last[0:1, 0:1] - cnt[...]

    def finish_y(d):
        from_face(d, 0).wait_recv()
        face_ref[0, 0, :, d * rows : (d + 1) * rows] = block_dot(vy.at[d - 2], 0, ry.at[d - 2], 0, c_x)

    def finish_x(d):
        @pl.when(origin_of(d))
        def _():
            for chunk in range(2):
                by_relay(d ^ 1, 1, chunk).wait_recv()

        @pl.when(jnp.logical_not(origin_of(d)))
        def _():
            from_face(d, 1).wait_recv()

        from_face(d, 0).wait_recv()
        face_ref[0, 0, :, d * rows : (d + 1) * rows] = block_dot(vx.at[d], 0, rx.at[d], 0, c_y)

    def face_zero(d):
        face_ref[0, 0, :, d * rows : (d + 1) * rows] = jnp.zeros((rows, rows), F32)

    for d in (2, 3, 0, 1):
        guarded(faces[d][0], lambda d=d: (finish_x if d < 2 else finish_y)(d))
        guarded(jnp.logical_not(faces[d][0]), lambda d=d: face_zero(d))

    def sent(d):
        to_face(d, 0).wait_send()
        if d < 2:

            @pl.when(origin_of(d))
            def _():
                for chunk in range(2):
                    by_relay(d, 0, chunk).wait_send()

            @pl.when(jnp.logical_not(origin_of(d)))
            def _():
                to_face(d, 1).wait_send()

    for d in range(4):
        guarded(faces[d][0], lambda d=d: sent(d))
        guarded(diagonals[d][0], lambda d=d: to_corner(d).wait_send())

    @pl.when(is_relay)
    def _():
        for chunk in range(2):
            by_relay(0, 1, chunk).wait_send()

    for r in range(rounds):
        guarded(iy + 2**r < n_y, lambda r=r: to_peer(r, 1).wait_send())
        if r + 1 < rounds:
            guarded(iy >= 2**r, lambda r=r: to_peer(r, 0).wait_send())


def hand_on(*refs):
    n = len(refs) // 2
    for i in range(n):
        refs[n + i][...] = refs[i][...]


def on_device(n_x, n_y, vectors, root_stiff, diag_coef, counts):
    rows, c_x, c_y, c_z = vectors.shape
    rounds = max(1, (n_y - 1).bit_length())
    vmem = pltpu.VMEM
    results = (
        jax.ShapeDtypeStruct((1, 1, rows, rows), F32),
        jax.ShapeDtypeStruct((1, 1, rows, 4 * rows), F32),
        jax.ShapeDtypeStruct((1, 1, rows, 4 * rows), F32),
        jax.ShapeDtypeStruct((1, 1), jnp.int32),
    )
    anywhere = pl.BlockSpec(memory_space=pl.ANY)
    outputs = pl.pallas_call(
        functools.partial(kernel, n_x, n_y),
        out_shape=results,
        in_specs=[anywhere] * 3 + [pl.BlockSpec(memory_space=pltpu.HBM)],
        out_specs=[pl.BlockSpec(memory_space=vmem)] * 4,
        scratch_shapes=[
            vmem((c_x, rows, c_y, c_z), BF16),
            vmem((c_x, c_y, c_z), F32),
            vmem((c_x, c_y, c_z), F32),
            vmem((1, 1), jnp.int32),
            vmem((c_x, rows * (c_y + 1) + 7, c_z), F32),
            vmem((c_x, c_y, rows, c_z), BF16),
            vmem((2, c_y, rows, c_z), BF16),
            vmem((c_x, rows, c_z), BF16),
            vmem((c_x, rows, c_z), BF16),
            vmem((c_x + 2, c_y + 2, rows, c_z), F32),
            vmem((2, c_y, rows, c_z), BF16),
            vmem((2, c_y, rows, c_z), BF16),
            vmem((2, c_x, rows, c_z), BF16),
            vmem((2, c_y, rows, c_z), BF16),
            vmem((2, c_x, rows, c_z), BF16),
            vmem((4, rows, c_z), BF16),
            vmem((2, c_y // 4, rows, c_z), BF16),
            vmem((rounds, 8, c_z), jnp.int32),
            vmem((8, c_z), jnp.int32),
            vmem((rounds, 2, 8, c_z), jnp.int32),
            pltpu.SemaphoreType.DMA((c_x + 3,)),
            pltpu.SemaphoreType.DMA((12,)),
            pltpu.SemaphoreType.DMA((12,)),
            pltpu.SemaphoreType.DMA((rounds, 2)),
            pltpu.SemaphoreType.DMA((rounds, 2)),
            pltpu.SemaphoreType.DMA((2, 2, 2)),
        ],
        compiler_params=pltpu.CompilerParams(
            collective_id=0, has_side_effects=True, vmem_limit_bytes=60 * 1024 * 1024
        ),
        cost_estimate=pl.CostEstimate(flops=600_000_000, bytes_accessed=5_000_000, transcendentals=0),
        name="coarse",
    )(vectors, root_stiff, diag_coef, counts)
    return pl.pallas_call(
        hand_on,
        out_shape=results,
        in_specs=[pl.BlockSpec(memory_space=vmem)] * len(results),
        out_specs=[pl.BlockSpec(memory_space=vmem)] * len(results),
        name="results",
    )(*outputs)


def solution(mesh):
    n_x, n_y = mesh.shape["sx"], mesh.shape["sy"]
    return jax.shard_map(
        functools.partial(on_device, n_x, n_y),
        mesh=mesh,
        in_specs=(
            P(None, "sx", "sy", None),
            P("sx", "sy", None),
            P("sx", "sy", None),
            P("sx", "sy"),
        ),
        out_specs=(
            P("sx", "sy", None, None),
            P("sx", "sy", None, None),
            P("sx", "sy", None, None),
            P("sx", "sy"),
        ),
        check_vma=False,
    )
```

```python
import functools

import jax
import jax.numpy as jnp
from jax import lax
from jax.experimental import pallas as pl
from jax.experimental.pallas import tpu as pltpu
from jax.sharding import PartitionSpec as P

MESH = pl.DeviceIdType.MESH
F32 = jnp.float32
BF16 = jnp.bfloat16


def row_dot(left, right):
    return lax.dot_general(left, right, (((1,), (1,)), ((), ())), preferred_element_type=F32)


def along_lanes(pieces):
    return jnp.concatenate(pieces, axis=1)


def block_dot(left_ref, left_start, right_ref, right_start, count):
    return row_dot(
        along_lanes([left_ref[left_start + i] for i in range(count)]),
        along_lanes([right_ref[right_start + i] for i in range(count)]),
    )


def kernel(
    n_x,
    n_y,
    vec_ref,
    rs_ref,
    dg_ref,
    cnt_ref,
    own_ref,
    face_ref,
    corner_ref,
    off_ref,
    vv,
    rs,
    dg,
    wide,
    mb,
    sx,
    sy0,
    sy1,
    zp,
    ab,
    vx,
    vy,
    rx,
    ry,
    rc,
    rr,
    cb,
    cr,
    load_sem,
    send_sem,
    recv_sem,
    csend_sem,
    crecv_sem,
    relay_sem,
):
    rows, c_x, c_y, c_z = vec_ref.shape
    pitch = c_y + 1
    ix, iy = lax.axis_index("sx"), lax.axis_index("sy")

    def load(x):
        return pltpu.make_async_copy(vec_ref.at[:, x], vv.at[x], load_sem.at[x])

    rs_load = pltpu.make_async_copy(rs_ref, rs, load_sem.at[c_x])
    dg_load = pltpu.make_async_copy(dg_ref, dg, load_sem.at[c_x + 1])
    rs_load.start()
    load(0).start()
    load(c_x - 1).start()
    for x in range(1, c_x - 1):
        load(x).start()
    dg_load.start()

    low_x, high_x = ix > 0, ix < n_x - 1
    low_y, high_y = iy > 0, iy < n_y - 1
    faces = [
        (low_x, (ix - 1, iy)),
        (high_x, (ix + 1, iy)),
        (low_y, (ix, iy - 1)),
        (high_y, (ix, iy + 1)),
    ]
    diagonals = [
        (low_x & low_y, (ix - 1, iy - 1)),
        (low_x & high_y, (ix - 1, iy + 1)),
        (high_x & low_y, (ix + 1, iy - 1)),
        (high_x & high_y, (ix + 1, iy + 1)),
    ]

    barrier = pltpu.get_barrier_semaphore()
    for there, device in faces + diagonals:

        @pl.when(there)
        def _(device=device):
            pl.semaphore_signal(barrier, inc=1, device_id=device, device_id_type=MESH)

    for far in range(2, n_y):

        @pl.when(iy >= far)
        def _(far=far):
            pl.semaphore_signal(barrier, inc=1, device_id=(ix, iy - far), device_id_type=MESH)

    across_low, across_high = n_x // 2 - 1, n_x // 2
    is_origin = (ix == across_low) | (ix == across_high)
    is_relay = (ix == 0) | (ix == n_x - 1)
    via_y = iy + 1 - 2 * lax.rem(iy, 2)
    origin_to = (jnp.where(ix == across_low, n_x - 1, 0), via_y)
    relay_to = (jnp.where(ix == 0, across_low, across_high), via_y)
    relay_from = (jnp.where(ix == 0, across_high, across_low), via_y)
    target_from = (jnp.where(ix == across_low, 0, n_x - 1), via_y)

    @pl.when(is_relay)
    def _():
        pl.semaphore_signal(barrier, inc=1, device_id=relay_from, device_id_type=MESH)

    @pl.when(is_origin)
    def _():
        pl.semaphore_signal(barrier, inc=1, device_id=target_from, device_id_type=MESH)

    greeted = sum(there.astype(jnp.int32) for there, _ in faces + diagonals)
    greeted = greeted + (is_relay | is_origin).astype(jnp.int32)
    greeted = greeted + jnp.maximum(n_y - 2 - iy, 0)

    lane_r = lax.broadcasted_iota(jnp.int32, (c_z, c_z), 0)
    lane_c = lax.broadcasted_iota(jnp.int32, (c_z, c_z), 1)
    apart = jnp.abs(lane_r - lane_c)
    smooth = jnp.where(apart == 0, 1.0, jnp.where(apart == 1, 0.5, 0.0)).astype(BF16)

    def zero_row(y, _):
        zp[0, y] = jnp.zeros((rows, c_z), F32)
        zp[c_x + 1, y] = jnp.zeros((rows, c_z), F32)
        return _

    lax.fori_loop(0, c_y + 2, zero_row, 0)
    for x in range(1, c_x + 1):
        zp[x, 0] = jnp.zeros((rows, c_z), F32)
        zp[x, c_y + 1] = jnp.zeros((rows, c_z), F32)

    count = cnt_ref[0, 0]
    cb[...] = jnp.full(cb.shape, count, jnp.int32)
    keep = lax.broadcasted_iota(jnp.int32, (rows, c_z), 0) < count

    def widen(x):
        load(x).wait()
        for a in range(rows):
            wide[x, a * pitch : a * pitch + c_y, :] = vv[x, a].astype(F32)

    def row(x, y):
        m = jnp.where(keep, wide[x, pl.ds(y, rows, stride=pitch), :], 0.0)
        return m, m * rs[x, y : y + 1, :]

    def smoothed(x, pieces):
        z = jnp.dot(jnp.concatenate(pieces, axis=0), smooth, preferred_element_type=F32)
        for y in range(c_y):
            zp[x + 1, y + 1] = z[y * rows : (y + 1) * rows]

    def scale(x):
        pieces = []
        for y in range(c_y):
            m, s = row(x, y)
            mb[x, y] = m.astype(BF16)
            pieces.append(s.astype(BF16))
        smoothed(x, pieces)

    rs_load.wait()
    for side, x in enumerate((0, c_x - 1)):
        widen(x)
        for y in range(c_y):
            m, s = row(x, y)
            mb[x, y] = m.astype(BF16)
            sx[side, y] = s.astype(BF16)

    def widen_step(x, _):
        widen(x)
        return _

    lax.fori_loop(1, c_x - 1, widen_step, 0)
    for x in range(c_x):
        sy0[x] = row(x, 0)[1].astype(BF16)
        sy1[x] = row(x, c_y - 1)[1].astype(BF16)

    pl.semaphore_wait(barrier, greeted)

    def to_face(d, part, to=None):
        opposite = d ^ 1
        if d < 2:
            piece = pl.ds(part * (c_y // 2), c_y // 2)
            src, dst = sx.at[d, piece], rx.at[opposite, piece]
        else:
            src, dst = (sy0, sy1)[d - 2], ry.at[opposite - 2]
        return pltpu.make_async_remote_copy(
            src_ref=src,
            dst_ref=dst,
            send_sem=send_sem.at[part * 2 + d if d < 2 else 2 + d],
            recv_sem=recv_sem.at[part * 2 + opposite if d < 2 else 2 + opposite],
            device_id=faces[d if to is None else to][1],
            device_id_type=MESH,
        )

    def from_face(d, part):
        return to_face(d ^ 1, part, d)

    def by_relay(d, leg, chunk):
        opposite = d ^ 1
        piece = pl.ds(c_y // 2 + chunk * (c_y // 4), c_y // 4)
        src, dst = [
            (sx.at[d, piece], rr.at[chunk]),
            (rr.at[chunk], rx.at[opposite, piece]),
        ][leg]
        return pltpu.make_async_remote_copy(
            src_ref=src,
            dst_ref=dst,
            send_sem=relay_sem.at[0, leg, chunk],
            recv_sem=relay_sem.at[1, leg, chunk],
            device_id=(origin_to, relay_to)[leg],
            device_id_type=MESH,
        )

    def to_corner(d, to=None):
        opposite = 3 - d
        side = (sy0, sy1)[d % 2]
        return pltpu.make_async_remote_copy(
            src_ref=side.at[(0, c_x - 1)[d // 2]],
            dst_ref=rc.at[opposite],
            send_sem=send_sem.at[8 + d],
            recv_sem=recv_sem.at[8 + opposite],
            device_id=diagonals[d if to is None else to][1],
            device_id_type=MESH,
        )

    def from_corner(d):
        return to_corner(3 - d, d)

    def to_peer(far):
        return pltpu.make_async_remote_copy(
            src_ref=cb,
            dst_ref=cr.at[far],
            send_sem=csend_sem.at[far],
            recv_sem=crecv_sem.at[far],
            device_id=(ix, iy + far),
            device_id_type=MESH,
        )

    def guarded(there, action):
        @pl.when(there)
        def _():
            action()

    def origin_of(d):
        return ix == (across_high, across_low)[d]

    def send_x(d):
        @pl.when(origin_of(d))
        def _():
            for chunk in range(2):
                by_relay(d, 0, chunk).start()

        to_face(d, 0).start()

        @pl.when(jnp.logical_not(origin_of(d)))
        def _():
            to_face(d, 1).start()

    for far in range(1, n_y):
        guarded(iy + far < n_y, lambda far=far: to_peer(far).start())
    for d in (1, 0):
        guarded(faces[d][0], lambda d=d: send_x(d))
    for d in (3, 2):
        guarded(faces[d][0], lambda d=d: to_face(d, 0).start())
    for d in range(4):
        guarded(diagonals[d][0], lambda d=d: to_corner(d).start())

    for side, x in enumerate((0, c_x - 1)):
        smoothed(x, [sx[side, y] for y in range(c_y)])

    def scale_step(x, _):
        scale(x)
        return _

    lax.fori_loop(1, c_x - 1, scale_step, 0)

    for side, x in enumerate((1, c_x)):
        for y in range(c_y):
            vx[side, y] = (
                -0.25 * ((zp[x, y] + zp[x, y + 2]) + 2.0 * zp[x, y + 1])
            ).astype(BF16)
    for side, y in enumerate((1, c_y)):
        for x in range(c_x):
            vy[side, x] = (
                -0.25 * ((zp[x, y] + zp[x + 2, y]) + 2.0 * zp[x + 1, y])
            ).astype(BF16)

    dg_load.wait()
    dg[...] = dg[...] + rs[...] * rs[...]
    rs[...] = rs[...] * 0.25

    def apply(x, slot):
        def across(y):
            near = zp[x + 1, y]
            return (zp[x, y] + near) + (near + zp[x + 2, y])

        here = across(1)
        before = here
        for y in range(c_y):
            ahead = across(y + 2)
            after = here + ahead
            m = mb[x, y].astype(F32)
            applied = dg[x, pl.ds(y, 1), :] * m - rs[x, pl.ds(y, 1), :] * (before + after)
            ab[slot, y] = applied.astype(BF16)
            here, before = ahead, after

    def product(x, slot):
        return block_dot(mb.at[x], 0, ab.at[slot], 0, c_y)

    apply(0, 0)

    def own_step(i, total):
        x = 2 * i
        total = total + product(x, 0)
        apply(x + 1, 1)
        total = total + product(x + 1, 1)
        apply(x + 2, 0)
        return total

    def hand_over(d, chunk):
        by_relay(d, 0, chunk).wait_recv()
        by_relay(d, 1, chunk).start()

    total = jnp.zeros((rows, rows), F32)
    for step in range(c_x // 2 - 1):
        total = lax.fori_loop(step, step + 1, own_step, total)
        if step < 2:
            guarded(ix == 0, lambda step=step: hand_over(0, step))
            guarded(ix == n_x - 1, lambda step=step: hand_over(1, step))
    total = total + product(c_x - 2, 0)
    apply(c_x - 1, 1)
    own_ref[0, 0] = total + product(c_x - 1, 1)

    for d in range(4):

        def corner_sum(d=d):
            from_corner(d).wait_recv()
            x, y = (0, c_x - 1)[d // 2], (0, c_y - 1)[d % 2]
            mine = (-0.25 * zp[x + 1, y + 1]).astype(BF16)
            corner_ref[0, 0, :, d * rows : (d + 1) * rows] = row_dot(mine, rc[d])

        def corner_zero(d=d):
            corner_ref[0, 0, :, d * rows : (d + 1) * rows] = jnp.zeros((rows, rows), F32)

        guarded(diagonals[d][0], corner_sum)
        guarded(jnp.logical_not(diagonals[d][0]), corner_zero)

    off_ref[...] = jnp.zeros(off_ref.shape, jnp.int32)
    for far in range(1, n_y):

        def earlier(far=far):
            to_peer(far).wait_recv()
            off_ref[...] += cr[far, 0:1, 0:1]

        guarded(iy >= far, earlier)

    def finish_y(d):
        from_face(d, 0).wait_recv()
        face_ref[0, 0, :, d * rows : (d + 1) * rows] = block_dot(vy.at[d - 2], 0, ry.at[d - 2], 0, c_x)

    half = c_y // 2

    def first_x(d):
        from_face(d, 0).wait_recv()
        face_ref[0, 0, :, d * rows : (d + 1) * rows] = block_dot(vx.at[d], 0, rx.at[d], 0, half)

    def last_x(d):
        @pl.when(origin_of(d))
        def _():
            for chunk in range(2):
                by_relay(d ^ 1, 1, chunk).wait_recv()

        @pl.when(jnp.logical_not(origin_of(d)))
        def _():
            from_face(d, 1).wait_recv()

        face_ref[0, 0, :, d * rows : (d + 1) * rows] += block_dot(vx.at[d], half, rx.at[d], half, half)

    def face_zero(d):
        face_ref[0, 0, :, d * rows : (d + 1) * rows] = jnp.zeros((rows, rows), F32)

    for d in range(4):
        guarded(jnp.logical_not(faces[d][0]), lambda d=d: face_zero(d))
    for d in (2, 3):
        guarded(faces[d][0], lambda d=d: finish_y(d))
    for d in (0, 1):
        guarded(faces[d][0], lambda d=d: first_x(d))
    for d in (0, 1):
        guarded(faces[d][0], lambda d=d: last_x(d))

    def sent(d):
        to_face(d, 0).wait_send()
        if d < 2:

            @pl.when(origin_of(d))
            def _():
                for chunk in range(2):
                    by_relay(d, 0, chunk).wait_send()

            @pl.when(jnp.logical_not(origin_of(d)))
            def _():
                to_face(d, 1).wait_send()

    for d in range(4):
        guarded(faces[d][0], lambda d=d: sent(d))
        guarded(diagonals[d][0], lambda d=d: to_corner(d).wait_send())

    @pl.when(is_relay)
    def _():
        for chunk in range(2):
            by_relay(0, 1, chunk).wait_send()

    for far in range(1, n_y):
        guarded(iy + far < n_y, lambda far=far: to_peer(far).wait_send())


def hand_on(own_in, face_in, corner_in, off_in, own_out, face_out, corner_out, off_out, sems):
    pairs = [(own_in, own_out), (face_in, face_out), (corner_in, corner_out)]
    copies = [pltpu.make_async_copy(a, b, sems.at[i]) for i, (a, b) in enumerate(pairs)]
    for copy in copies:
        copy.start()
    off_out[...] = off_in[...]
    for copy in copies:
        copy.wait()


def on_device(n_x, n_y, vectors, root_stiff, diag_coef, counts):
    rows, c_x, c_y, c_z = vectors.shape
    vmem = pltpu.VMEM
    results = (
        jax.ShapeDtypeStruct((1, 1, rows, rows), F32),
        jax.ShapeDtypeStruct((1, 1, rows, 4 * rows), F32),
        jax.ShapeDtypeStruct((1, 1, rows, 4 * rows), F32),
        jax.ShapeDtypeStruct((1, 1), jnp.int32),
    )
    anywhere = pl.BlockSpec(memory_space=pl.ANY)
    outputs = pl.pallas_call(
        functools.partial(kernel, n_x, n_y),
        out_shape=results,
        in_specs=[anywhere] * 3 + [pl.BlockSpec(memory_space=pltpu.SMEM)],
        out_specs=[pl.BlockSpec(memory_space=vmem)] * 4,
        scratch_shapes=[
            vmem((c_x, rows, c_y, c_z), BF16),
            vmem((c_x, c_y, c_z), F32),
            vmem((c_x, c_y, c_z), F32),
            vmem((c_x, rows * (c_y + 1) + 7, c_z), F32),
            vmem((c_x, c_y, rows, c_z), BF16),
            vmem((2, c_y, rows, c_z), BF16),
            vmem((c_x, rows, c_z), BF16),
            vmem((c_x, rows, c_z), BF16),
            vmem((c_x + 2, c_y + 2, rows, c_z), F32),
            vmem((2, c_y, rows, c_z), BF16),
            vmem((2, c_y, rows, c_z), BF16),
            vmem((2, c_x, rows, c_z), BF16),
            vmem((2, c_y, rows, c_z), BF16),
            vmem((2, c_x, rows, c_z), BF16),
            vmem((4, rows, c_z), BF16),
            vmem((2, c_y // 4, rows, c_z), BF16),
            vmem((8, c_z), jnp.int32),
            vmem((n_y, 8, c_z), jnp.int32),
            pltpu.SemaphoreType.DMA((c_x + 2,)),
            pltpu.SemaphoreType.DMA((12,)),
            pltpu.SemaphoreType.DMA((12,)),
            pltpu.SemaphoreType.DMA((n_y,)),
            pltpu.SemaphoreType.DMA((n_y,)),
            pltpu.SemaphoreType.DMA((2, 2, 2)),
        ],
        compiler_params=pltpu.CompilerParams(
            collective_id=0, has_side_effects=True, vmem_limit_bytes=55040 * 1024
        ),
        cost_estimate=pl.CostEstimate(flops=600_000_000, bytes_accessed=5_000_000, transcendentals=0),
        name="coarse",
    )(vectors, root_stiff, diag_coef, counts)
    return pl.pallas_call(
        hand_on,
        out_shape=results,
        in_specs=[anywhere] * 3 + [pl.BlockSpec(memory_space=vmem)],
        out_specs=[anywhere] * 3 + [pl.BlockSpec(memory_space=vmem)],
        scratch_shapes=[pltpu.SemaphoreType.DMA((3,))],
        name="results",
        compiler_params=pltpu.CompilerParams(vmem_limit_bytes=4 * 1024 * 1024),
    )(*outputs)


def solution(mesh):
    n_x, n_y = mesh.shape["sx"], mesh.shape["sy"]
    return jax.shard_map(
        functools.partial(on_device, n_x, n_y),
        mesh=mesh,
        in_specs=(
            P(None, "sx", "sy", None),
            P("sx", "sy", None),
            P("sx", "sy", None),
            P("sx", "sy"),
        ),
        out_specs=(
            P("sx", "sy", None, None),
            P("sx", "sy", None, None),
            P("sx", "sy", None, None),
            P("sx", "sy"),
        ),
        check_vma=False,
    )
```

```python
import functools

import jax
import jax.numpy as jnp
from jax import lax
from jax.experimental import pallas as pl
from jax.experimental.pallas import tpu as pltpu
from jax.sharding import PartitionSpec as P

MESH = pl.DeviceIdType.MESH
F32 = jnp.float32
BF16 = jnp.bfloat16


def row_dot(left, right):
    return lax.dot_general(left, right, (((1,), (1,)), ((), ())), preferred_element_type=F32)


def along_lanes(pieces):
    return jnp.concatenate(pieces, axis=1)


def block_dot(left_ref, left_start, right_ref, right_start, count):
    return row_dot(
        along_lanes([left_ref[left_start + i] for i in range(count)]),
        along_lanes([right_ref[right_start + i] for i in range(count)]),
    )


def kernel(
    n_x,
    n_y,
    vec_ref,
    rs_ref,
    dg_ref,
    cnt_ref,
    own_ref,
    face_ref,
    corner_ref,
    off_ref,
    vv,
    rs,
    dg,
    wide,
    mb,
    sx,
    sy0,
    sy1,
    zp,
    ab,
    vx,
    vy,
    rx,
    ry,
    rc,
    rr,
    vc,
    cb,
    cr,
    load_sem,
    send_sem,
    recv_sem,
    csend_sem,
    crecv_sem,
    relay_sem,
):
    rows, c_x, c_y, c_z = vec_ref.shape
    pitch = c_y + 1
    ix, iy = lax.axis_index("sx"), lax.axis_index("sy")

    def guarded(there, action):
        @pl.when(there)
        def _():
            action()

    low_x, high_x = ix > 0, ix < n_x - 1
    low_y, high_y = iy > 0, iy < n_y - 1
    faces = [
        (low_x, (ix - 1, iy)),
        (high_x, (ix + 1, iy)),
        (low_y, (ix, iy - 1)),
        (high_y, (ix, iy + 1)),
    ]
    diagonals = [
        (low_x & low_y, (ix - 1, iy - 1)),
        (low_x & high_y, (ix - 1, iy + 1)),
        (high_x & low_y, (ix + 1, iy - 1)),
        (high_x & high_y, (ix + 1, iy + 1)),
    ]

    barrier = pltpu.get_barrier_semaphore()
    for there, device in faces + diagonals:

        @pl.when(there)
        def _(device=device):
            pl.semaphore_signal(barrier, inc=1, device_id=device, device_id_type=MESH)

    for far in range(2, n_y):

        @pl.when(iy >= far)
        def _(far=far):
            pl.semaphore_signal(barrier, inc=1, device_id=(ix, iy - far), device_id_type=MESH)

    across_low, across_high = n_x // 2 - 1, n_x // 2
    is_origin = (ix == across_low) | (ix == across_high)
    is_relay = (ix == 0) | (ix == n_x - 1)
    via_y = iy + 1 - 2 * lax.rem(iy, 2)
    origin_to = (jnp.where(ix == across_low, n_x - 1, 0), via_y)
    relay_to = (jnp.where(ix == 0, across_low, across_high), via_y)
    relay_from = (jnp.where(ix == 0, across_high, across_low), via_y)
    target_from = (jnp.where(ix == across_low, 0, n_x - 1), via_y)

    @pl.when(is_relay)
    def _():
        pl.semaphore_signal(barrier, inc=1, device_id=relay_from, device_id_type=MESH)

    @pl.when(is_origin)
    def _():
        pl.semaphore_signal(barrier, inc=1, device_id=target_from, device_id_type=MESH)

    def load(x):
        return pltpu.make_async_copy(vec_ref.at[:, x], vv.at[x], load_sem.at[x])

    rs_load = pltpu.make_async_copy(rs_ref, rs, load_sem.at[c_x])
    dg_load = pltpu.make_async_copy(dg_ref, dg, load_sem.at[c_x + 1])
    rs_load.start()
    load(0).start()
    load(c_x - 1).start()
    for x in range(1, c_x - 1):
        load(x).start()
    dg_load.start()

    greeted = sum(there.astype(jnp.int32) for there, _ in faces + diagonals)
    greeted = greeted + (is_relay | is_origin).astype(jnp.int32)
    greeted = greeted + jnp.maximum(n_y - 2 - iy, 0)

    def zero_layers(ref):
        def step(i, _):
            ref[i] = jnp.zeros((rows, c_z), BF16)
            return _

        lax.fori_loop(0, ref.shape[0], step, 0)

    for d in range(4):
        layers = rx.at[d] if d < 2 else ry.at[d - 2]
        guarded(jnp.logical_not(faces[d][0]), lambda layers=layers: zero_layers(layers))

        @pl.when(jnp.logical_not(diagonals[d][0]))
        def _(d=d):
            rc[d] = jnp.zeros((rows, c_z), BF16)

    lane_r = lax.broadcasted_iota(jnp.int32, (c_z, c_z), 0)
    lane_c = lax.broadcasted_iota(jnp.int32, (c_z, c_z), 1)
    apart = jnp.abs(lane_r - lane_c)
    smooth = jnp.where(apart == 0, 1.0, jnp.where(apart == 1, 0.5, 0.0)).astype(BF16)

    def zero_row(y, _):
        zp[0, y] = jnp.zeros((rows, c_z), F32)
        zp[c_x + 1, y] = jnp.zeros((rows, c_z), F32)
        return _

    lax.fori_loop(0, c_y + 2, zero_row, 0)
    for x in range(1, c_x + 1):
        zp[x, 0] = jnp.zeros((rows, c_z), F32)
        zp[x, c_y + 1] = jnp.zeros((rows, c_z), F32)

    count = cnt_ref[0, 0]
    cb[...] = jnp.full(cb.shape, count, jnp.int32)
    keep = lax.broadcasted_iota(jnp.int32, (rows, c_z), 0) < count

    def widen(x):
        load(x).wait()
        for a in range(rows):
            wide[x, a * pitch : a * pitch + c_y, :] = vv[x, a].astype(F32)

    def row(x, y):
        m = jnp.where(keep, wide[x, pl.ds(y, rows, stride=pitch), :], 0.0)
        return m, m * rs[x, y : y + 1, :]

    def smoothed(x, pieces):
        z = jnp.dot(jnp.concatenate(pieces, axis=0), smooth, preferred_element_type=F32)
        for y in range(c_y):
            zp[x + 1, y + 1] = z[y * rows : (y + 1) * rows]

    def scale(x):
        pieces = []
        for y in range(c_y):
            m, s = row(x, y)
            mb[x, y] = m.astype(BF16)
            pieces.append(s.astype(BF16))
        smoothed(x, pieces)

    rs_load.wait()
    for side, x in enumerate((0, c_x - 1)):
        widen(x)
        for y in range(c_y):
            m, s = row(x, y)
            mb[x, y] = m.astype(BF16)
            sx[side, y] = s.astype(BF16)

    def widen_step(x, _):
        widen(x)
        return _

    lax.fori_loop(1, c_x - 1, widen_step, 0)
    for x in range(c_x):
        sy0[x] = row(x, 0)[1].astype(BF16)
        sy1[x] = row(x, c_y - 1)[1].astype(BF16)

    pl.semaphore_wait(barrier, greeted)

    def to_face(d, part, to=None):
        opposite = d ^ 1
        if d < 2:
            piece = pl.ds(part * (c_y // 2), c_y // 2)
            src, dst = sx.at[d, piece], rx.at[opposite, piece]
        else:
            src, dst = (sy0, sy1)[d - 2], ry.at[opposite - 2]
        return pltpu.make_async_remote_copy(
            src_ref=src,
            dst_ref=dst,
            send_sem=send_sem.at[part * 2 + d if d < 2 else 2 + d],
            recv_sem=recv_sem.at[part * 2 + opposite if d < 2 else 2 + opposite],
            device_id=faces[d if to is None else to][1],
            device_id_type=MESH,
        )

    def from_face(d, part):
        return to_face(d ^ 1, part, d)

    def by_relay(d, leg, chunk):
        opposite = d ^ 1
        piece = pl.ds(c_y // 2 + chunk * (c_y // 4), c_y // 4)
        src, dst = [
            (sx.at[d, piece], rr.at[chunk]),
            (rr.at[chunk], rx.at[opposite, piece]),
        ][leg]
        return pltpu.make_async_remote_copy(
            src_ref=src,
            dst_ref=dst,
            send_sem=relay_sem.at[0, leg, chunk],
            recv_sem=relay_sem.at[1, leg, chunk],
            device_id=(origin_to, relay_to)[leg],
            device_id_type=MESH,
        )

    def to_corner(d, to=None):
        opposite = 3 - d
        side = (sy0, sy1)[d % 2]
        return pltpu.make_async_remote_copy(
            src_ref=side.at[(0, c_x - 1)[d // 2]],
            dst_ref=rc.at[opposite],
            send_sem=send_sem.at[8 + d],
            recv_sem=recv_sem.at[8 + opposite],
            device_id=diagonals[d if to is None else to][1],
            device_id_type=MESH,
        )

    def from_corner(d):
        return to_corner(3 - d, d)

    def to_peer(far):
        return pltpu.make_async_remote_copy(
            src_ref=cb,
            dst_ref=cr.at[far],
            send_sem=csend_sem.at[far],
            recv_sem=crecv_sem.at[far],
            device_id=(ix, iy + far),
            device_id_type=MESH,
        )

    def origin_of(d):
        return ix == (across_high, across_low)[d]

    def send_x(d):
        @pl.when(origin_of(d))
        def _():
            for chunk in range(2):
                by_relay(d, 0, chunk).start()

        to_face(d, 0).start()

        @pl.when(jnp.logical_not(origin_of(d)))
        def _():
            to_face(d, 1).start()

    for d in range(4):
        guarded(diagonals[d][0], lambda d=d: to_corner(d).start())
    for d in (1, 0):
        guarded(faces[d][0], lambda d=d: send_x(d))
    for d in (3, 2):
        guarded(faces[d][0], lambda d=d: to_face(d, 0).start())
    for far in range(1, n_y):
        guarded(iy + far < n_y, lambda far=far: to_peer(far).start())

    for side, x in enumerate((0, c_x - 1)):
        smoothed(x, [sx[side, y] for y in range(c_y)])

    def scale_step(x, _):
        scale(x)
        return _

    lax.fori_loop(1, c_x - 1, scale_step, 0)

    for side, x in enumerate((1, c_x)):
        for y in range(c_y):
            vx[side, y] = (
                -0.25 * ((zp[x, y] + zp[x, y + 2]) + 2.0 * zp[x, y + 1])
            ).astype(BF16)
    for side, y in enumerate((1, c_y)):
        for x in range(c_x):
            vy[side, x] = (
                -0.25 * ((zp[x, y] + zp[x + 2, y]) + 2.0 * zp[x + 1, y])
            ).astype(BF16)

    dg_load.wait()
    dg[...] = dg[...] + rs[...] * rs[...]
    rs[...] = rs[...] * 0.25

    def apply(x, slot):
        def across(y):
            near = zp[x + 1, y]
            return (zp[x, y] + near) + (near + zp[x + 2, y])

        here = across(1)
        before = here
        for y in range(c_y):
            ahead = across(y + 2)
            after = here + ahead
            m = mb[x, y].astype(F32)
            applied = dg[x, pl.ds(y, 1), :] * m - rs[x, pl.ds(y, 1), :] * (before + after)
            ab[slot, y] = applied.astype(BF16)
            here, before = ahead, after

    def product(x, slot):
        return block_dot(mb.at[x], 0, ab.at[slot], 0, c_y)

    apply(0, 0)

    def own_step(i, total):
        x = 2 * i
        total = total + product(x, 0)
        apply(x + 1, 1)
        total = total + product(x + 1, 1)
        apply(x + 2, 0)
        return total

    def hand_over(d, chunk):
        by_relay(d, 0, chunk).wait_recv()
        by_relay(d, 1, chunk).start()

    total = jnp.zeros((rows, rows), F32)
    for step in range(c_x // 2 - 1):
        total = lax.fori_loop(step, step + 1, own_step, total)
        if step < 2:
            guarded(ix == 0, lambda step=step: hand_over(0, step))
            guarded(ix == n_x - 1, lambda step=step: hand_over(1, step))
    total = total + product(c_x - 2, 0)
    apply(c_x - 1, 1)
    own_ref[0, 0] = total + product(c_x - 1, 1)

    for d in range(4):
        x, y = (0, c_x - 1)[d // 2], (0, c_y - 1)[d % 2]
        vc[d] = (-0.25 * zp[x + 1, y + 1]).astype(BF16)

    off_ref[...] = jnp.zeros(off_ref.shape, jnp.int32)
    for far in range(1, n_y):

        def earlier(far=far):
            to_peer(far).wait_recv()
            off_ref[...] += cr[far, 0:1, 0:1]

        guarded(iy >= far, earlier)

    def arrived_x(d):
        from_face(d, 0).wait_recv()

        @pl.when(origin_of(d))
        def _():
            for chunk in range(2):
                by_relay(d ^ 1, 1, chunk).wait_recv()

        @pl.when(jnp.logical_not(origin_of(d)))
        def _():
            from_face(d, 1).wait_recv()

    for d in range(4):
        guarded(diagonals[d][0], lambda d=d: from_corner(d).wait_recv())
    for d in (2, 3):
        guarded(faces[d][0], lambda d=d: from_face(d, 0).wait_recv())
    for d in (0, 1):
        guarded(faces[d][0], lambda d=d: arrived_x(d))
    products = [block_dot(vx.at[d], 0, rx.at[d], 0, c_y) for d in range(2)]
    products += [block_dot(vy.at[d], 0, ry.at[d], 0, c_x) for d in range(2)]
    face_ref[0, 0] = along_lanes(products)
    corner_ref[0, 0] = along_lanes([row_dot(vc[d], rc[d]) for d in range(4)])

    def sent(d):
        to_face(d, 0).wait_send()
        if d < 2:

            @pl.when(origin_of(d))
            def _():
                for chunk in range(2):
                    by_relay(d, 0, chunk).wait_send()

            @pl.when(jnp.logical_not(origin_of(d)))
            def _():
                to_face(d, 1).wait_send()

    for d in range(4):
        guarded(faces[d][0], lambda d=d: sent(d))
        guarded(diagonals[d][0], lambda d=d: to_corner(d).wait_send())

    @pl.when(is_relay)
    def _():
        for chunk in range(2):
            by_relay(0, 1, chunk).wait_send()

    for far in range(1, n_y):
        guarded(iy + far < n_y, lambda far=far: to_peer(far).wait_send())


def hand_on(own_in, face_in, corner_in, off_in, own_out, face_out, corner_out, off_out, sems):
    pairs = [(own_in, own_out), (face_in, face_out), (corner_in, corner_out)]
    copies = [pltpu.make_async_copy(a, b, sems.at[i]) for i, (a, b) in enumerate(pairs)]
    for copy in copies:
        copy.start()
    off_out[...] = off_in[...]
    for copy in copies:
        copy.wait()


def on_device(n_x, n_y, vectors, root_stiff, diag_coef, counts):
    rows, c_x, c_y, c_z = vectors.shape
    vmem = pltpu.VMEM
    results = (
        jax.ShapeDtypeStruct((1, 1, rows, rows), F32),
        jax.ShapeDtypeStruct((1, 1, rows, 4 * rows), F32),
        jax.ShapeDtypeStruct((1, 1, rows, 4 * rows), F32),
        jax.ShapeDtypeStruct((1, 1), jnp.int32),
    )
    anywhere = pl.BlockSpec(memory_space=pl.ANY)
    outputs = pl.pallas_call(
        functools.partial(kernel, n_x, n_y),
        out_shape=results,
        in_specs=[anywhere] * 3 + [pl.BlockSpec(memory_space=pltpu.SMEM)],
        out_specs=[pl.BlockSpec(memory_space=vmem)] * 4,
        scratch_shapes=[
            vmem((c_x, rows, c_y, c_z), BF16),
            vmem((c_x, c_y, c_z), F32),
            vmem((c_x, c_y, c_z), F32),
            vmem((c_x, rows * (c_y + 1) + 7, c_z), F32),
            vmem((c_x, c_y, rows, c_z), BF16),
            vmem((2, c_y, rows, c_z), BF16),
            vmem((c_x, rows, c_z), BF16),
            vmem((c_x, rows, c_z), BF16),
            vmem((c_x + 2, c_y + 2, rows, c_z), F32),
            vmem((2, c_y, rows, c_z), BF16),
            vmem((2, c_y, rows, c_z), BF16),
            vmem((2, c_x, rows, c_z), BF16),
            vmem((2, c_y, rows, c_z), BF16),
            vmem((2, c_x, rows, c_z), BF16),
            vmem((4, rows, c_z), BF16),
            vmem((2, c_y // 4, rows, c_z), BF16),
            vmem((4, rows, c_z), BF16),
            vmem((8, c_z), jnp.int32),
            vmem((n_y, 8, c_z), jnp.int32),
            pltpu.SemaphoreType.DMA((c_x + 2,)),
            pltpu.SemaphoreType.DMA((12,)),
            pltpu.SemaphoreType.DMA((12,)),
            pltpu.SemaphoreType.DMA((n_y,)),
            pltpu.SemaphoreType.DMA((n_y,)),
            pltpu.SemaphoreType.DMA((2, 2, 2)),
        ],
        compiler_params=pltpu.CompilerParams(
            collective_id=0, has_side_effects=True, vmem_limit_bytes=55040 * 1024
        ),
        cost_estimate=pl.CostEstimate(flops=600_000_000, bytes_accessed=5_000_000, transcendentals=0),
        name="coarse",
    )(vectors, root_stiff, diag_coef, counts)
    return pl.pallas_call(
        hand_on,
        out_shape=results,
        in_specs=[anywhere] * 3 + [pl.BlockSpec(memory_space=vmem)],
        out_specs=[anywhere] * 3 + [pl.BlockSpec(memory_space=vmem)],
        scratch_shapes=[pltpu.SemaphoreType.DMA((3,))],
        name="results",
        compiler_params=pltpu.CompilerParams(vmem_limit_bytes=4 * 1024 * 1024),
    )(*outputs)


def solution(mesh):
    n_x, n_y = mesh.shape["sx"], mesh.shape["sy"]
    return jax.shard_map(
        functools.partial(on_device, n_x, n_y),
        mesh=mesh,
        in_specs=(
            P(None, "sx", "sy", None),
            P("sx", "sy", None),
            P("sx", "sy", None),
            P("sx", "sy"),
        ),
        out_specs=(
            P("sx", "sy", None, None),
            P("sx", "sy", None, None),
            P("sx", "sy", None, None),
            P("sx", "sy"),
        ),
        check_vma=False,
    )
```

```python
import functools

import jax
import jax.numpy as jnp
from jax import lax
from jax.experimental import pallas as pl
from jax.experimental.pallas import tpu as pltpu
from jax.sharding import PartitionSpec as P

MESH = pl.DeviceIdType.MESH
F32 = jnp.float32
BF16 = jnp.bfloat16


def row_dot(left, right):
    return lax.dot_general(left, right, (((1,), (1,)), ((), ())), preferred_element_type=F32)


def along_lanes(pieces):
    return jnp.concatenate(pieces, axis=1)


def block_dot(left_ref, left_start, right_ref, right_start, count):
    return row_dot(
        along_lanes([left_ref[left_start + i] for i in range(count)]),
        along_lanes([right_ref[right_start + i] for i in range(count)]),
    )


def kernel(
    n_x,
    n_y,
    vec_ref,
    rs_ref,
    dg_ref,
    cnt_ref,
    own_ref,
    face_ref,
    corner_ref,
    off_ref,
    vv,
    rs,
    dg,
    wide,
    mb,
    sx,
    sy0,
    sy1,
    zp,
    ab,
    vx,
    vy,
    rx,
    ry,
    rc,
    rr,
    vc,
    cb,
    cr,
    load_sem,
    send_sem,
    recv_sem,
    csend_sem,
    crecv_sem,
    relay_sem,
):
    rows, c_x, c_y, c_z = vec_ref.shape
    pitch = c_y + 1
    ix, iy = lax.axis_index("sx"), lax.axis_index("sy")

    def guarded(there, action):
        @pl.when(there)
        def _():
            action()

    low_x, high_x = ix > 0, ix < n_x - 1
    low_y, high_y = iy > 0, iy < n_y - 1
    faces = [
        (low_x, (ix - 1, iy)),
        (high_x, (ix + 1, iy)),
        (low_y, (ix, iy - 1)),
        (high_y, (ix, iy + 1)),
    ]
    diagonals = [
        (low_x & low_y, (ix - 1, iy - 1)),
        (low_x & high_y, (ix - 1, iy + 1)),
        (high_x & low_y, (ix + 1, iy - 1)),
        (high_x & high_y, (ix + 1, iy + 1)),
    ]

    barrier = pltpu.get_barrier_semaphore()
    for there, device in faces + diagonals:

        @pl.when(there)
        def _(device=device):
            pl.semaphore_signal(barrier, inc=1, device_id=device, device_id_type=MESH)

    for far in range(2, n_y):

        @pl.when(iy >= far)
        def _(far=far):
            pl.semaphore_signal(barrier, inc=1, device_id=(ix, iy - far), device_id_type=MESH)

    across_low, across_high = n_x // 2 - 1, n_x // 2
    is_origin = (ix == across_low) | (ix == across_high)
    is_relay = (ix == 0) | (ix == n_x - 1)
    via_y = iy + 1 - 2 * lax.rem(iy, 2)
    origin_to = (jnp.where(ix == across_low, n_x - 1, 0), via_y)
    relay_to = (jnp.where(ix == 0, across_low, across_high), via_y)
    relay_from = (jnp.where(ix == 0, across_high, across_low), via_y)
    target_from = (jnp.where(ix == across_low, 0, n_x - 1), via_y)

    @pl.when(is_relay)
    def _():
        pl.semaphore_signal(barrier, inc=1, device_id=relay_from, device_id_type=MESH)

    @pl.when(is_origin)
    def _():
        pl.semaphore_signal(barrier, inc=1, device_id=target_from, device_id_type=MESH)

    def load(x):
        return pltpu.make_async_copy(vec_ref.at[:, x], vv.at[x], load_sem.at[x])

    rs_load = pltpu.make_async_copy(rs_ref, rs, load_sem.at[c_x])
    dg_load = pltpu.make_async_copy(dg_ref, dg, load_sem.at[c_x + 1])
    rs_load.start()
    load(0).start()
    load(c_x - 1).start()
    for x in range(1, c_x - 1):
        load(x).start()
    dg_load.start()

    greeted = sum(there.astype(jnp.int32) for there, _ in faces + diagonals)
    greeted = greeted + (is_relay | is_origin).astype(jnp.int32)
    greeted = greeted + jnp.maximum(n_y - 2 - iy, 0)

    def zero_layers(ref):
        def step(i, _):
            ref[i] = jnp.zeros((rows, c_z), BF16)
            return _

        lax.fori_loop(0, ref.shape[0], step, 0)

    for d in range(4):
        layers = rx.at[d] if d < 2 else ry.at[d - 2]
        guarded(jnp.logical_not(faces[d][0]), lambda layers=layers: zero_layers(layers))

        @pl.when(jnp.logical_not(diagonals[d][0]))
        def _(d=d):
            rc[d] = jnp.zeros((rows, c_z), BF16)

    lane_r = lax.broadcasted_iota(jnp.int32, (c_z, c_z), 0)
    lane_c = lax.broadcasted_iota(jnp.int32, (c_z, c_z), 1)
    apart = jnp.abs(lane_r - lane_c)
    smooth = jnp.where(apart == 0, 1.0, jnp.where(apart == 1, 0.5, 0.0)).astype(BF16)

    def zero_row(y, _):
        zp[0, y] = jnp.zeros((rows, c_z), F32)
        zp[c_x + 1, y] = jnp.zeros((rows, c_z), F32)
        return _

    lax.fori_loop(0, c_y + 2, zero_row, 0)
    for x in range(1, c_x + 1):
        zp[x, 0] = jnp.zeros((rows, c_z), F32)
        zp[x, c_y + 1] = jnp.zeros((rows, c_z), F32)

    count = cnt_ref[0, 0]
    cb[...] = jnp.full(cb.shape, count, jnp.int32)
    keep = lax.broadcasted_iota(jnp.int32, (rows, c_z), 0) < count

    def widen(x):
        load(x).wait()
        for a in range(rows):
            wide[x, a * pitch : a * pitch + c_y, :] = vv[x, a].astype(F32)

    def row(x, y):
        m = jnp.where(keep, wide[x, pl.ds(y, rows, stride=pitch), :], 0.0)
        return m, m * rs[x, y : y + 1, :]

    def smoothed(x, pieces):
        z = jnp.dot(jnp.concatenate(pieces, axis=0), smooth, preferred_element_type=F32)
        for y in range(c_y):
            zp[x + 1, y + 1] = z[y * rows : (y + 1) * rows]

    def scale(x):
        pieces = []
        for y in range(c_y):
            m, s = row(x, y)
            mb[x, y] = m.astype(BF16)
            pieces.append(s.astype(BF16))
        smoothed(x, pieces)

    rs_load.wait()
    for side, x in enumerate((0, c_x - 1)):
        widen(x)
        for y in range(c_y):
            m, s = row(x, y)
            mb[x, y] = m.astype(BF16)
            sx[side, y] = s.astype(BF16)

    def widen_step(x, _):
        widen(x)
        return _

    lax.fori_loop(1, c_x - 1, widen_step, 0)
    for x in range(c_x):
        sy0[x] = row(x, 0)[1].astype(BF16)
        sy1[x] = row(x, c_y - 1)[1].astype(BF16)

    pl.semaphore_wait(barrier, greeted)

    def to_face(d, part, to=None):
        opposite = d ^ 1
        if d < 2:
            piece = pl.ds(part * (c_y // 2), c_y // 2)
            src, dst = sx.at[d, piece], rx.at[opposite, piece]
        else:
            src, dst = (sy0, sy1)[d - 2], ry.at[opposite - 2]
        return pltpu.make_async_remote_copy(
            src_ref=src,
            dst_ref=dst,
            send_sem=send_sem.at[part * 2 + d if d < 2 else 2 + d],
            recv_sem=recv_sem.at[part * 2 + opposite if d < 2 else 2 + opposite],
            device_id=faces[d if to is None else to][1],
            device_id_type=MESH,
        )

    def from_face(d, part):
        return to_face(d ^ 1, part, d)

    def by_relay(d, leg, chunk):
        opposite = d ^ 1
        piece = pl.ds(c_y // 2 + chunk * (c_y // 4), c_y // 4)
        src, dst = [
            (sx.at[d, piece], rr.at[chunk]),
            (rr.at[chunk], rx.at[opposite, piece]),
        ][leg]
        return pltpu.make_async_remote_copy(
            src_ref=src,
            dst_ref=dst,
            send_sem=relay_sem.at[0, leg, chunk],
            recv_sem=relay_sem.at[1, leg, chunk],
            device_id=(origin_to, relay_to)[leg],
            device_id_type=MESH,
        )

    def to_corner(d, to=None):
        opposite = 3 - d
        side = (sy0, sy1)[d % 2]
        return pltpu.make_async_remote_copy(
            src_ref=side.at[(0, c_x - 1)[d // 2]],
            dst_ref=rc.at[opposite],
            send_sem=send_sem.at[8 + d],
            recv_sem=recv_sem.at[8 + opposite],
            device_id=diagonals[d if to is None else to][1],
            device_id_type=MESH,
        )

    def from_corner(d):
        return to_corner(3 - d, d)

    def to_peer(far):
        return pltpu.make_async_remote_copy(
            src_ref=cb,
            dst_ref=cr.at[far],
            send_sem=csend_sem.at[far],
            recv_sem=crecv_sem.at[far],
            device_id=(ix, iy + far),
            device_id_type=MESH,
        )

    def origin_of(d):
        return ix == (across_high, across_low)[d]

    def send_x(d):
        @pl.when(origin_of(d))
        def _():
            for chunk in range(2):
                by_relay(d, 0, chunk).start()

        to_face(d, 0).start()

        @pl.when(jnp.logical_not(origin_of(d)))
        def _():
            to_face(d, 1).start()

    for d in range(4):
        guarded(diagonals[d][0], lambda d=d: to_corner(d).start())
    for d in (1, 0):
        guarded(faces[d][0], lambda d=d: send_x(d))
    for d in (3, 2):
        guarded(faces[d][0], lambda d=d: to_face(d, 0).start())
    for far in range(1, n_y):
        guarded(iy + far < n_y, lambda far=far: to_peer(far).start())

    for side, x in enumerate((0, c_x - 1)):
        smoothed(x, [sx[side, y] for y in range(c_y)])

    def scale_step(x, _):
        scale(x)
        return _

    lax.fori_loop(1, c_x - 1, scale_step, 0)

    for side, x in enumerate((1, c_x)):
        for y in range(c_y):
            vx[side, y] = (
                -0.25 * ((zp[x, y] + zp[x, y + 2]) + 2.0 * zp[x, y + 1])
            ).astype(BF16)
    for side, y in enumerate((1, c_y)):
        for x in range(c_x):
            vy[side, x] = (
                -0.25 * ((zp[x, y] + zp[x + 2, y]) + 2.0 * zp[x + 1, y])
            ).astype(BF16)

    dg_load.wait()
    dg[...] = dg[...] + rs[...] * rs[...]
    rs[...] = rs[...] * 0.25

    def apply(x, slot):
        def across(y):
            near = zp[x + 1, y]
            return (zp[x, y] + near) + (near + zp[x + 2, y])

        here = across(1)
        before = here
        for y in range(c_y):
            ahead = across(y + 2)
            after = here + ahead
            m = mb[x, y].astype(F32)
            applied = dg[x, pl.ds(y, 1), :] * m - rs[x, pl.ds(y, 1), :] * (before + after)
            ab[slot, y] = applied.astype(BF16)
            here, before = ahead, after

    def product(x, slot):
        return block_dot(mb.at[x], 0, ab.at[slot], 0, c_y)

    apply(0, 0)

    def own_step(i, total):
        x = 2 * i
        total = total + product(x, 0)
        apply(x + 1, 1)
        total = total + product(x + 1, 1)
        apply(x + 2, 0)
        return total

    def hand_over(d, chunk):
        by_relay(d, 0, chunk).wait_recv()
        by_relay(d, 1, chunk).start()

    total = jnp.zeros((rows, rows), F32)
    for step in range(c_x // 2 - 1):
        total = lax.fori_loop(step, step + 1, own_step, total)
        if step < 2:
            guarded(ix == 0, lambda step=step: hand_over(0, step))
            guarded(ix == n_x - 1, lambda step=step: hand_over(1, step))
    total = total + product(c_x - 2, 0)
    apply(c_x - 1, 1)
    own_ref[0, 0] = total + product(c_x - 1, 1)

    for d in range(4):
        x, y = (0, c_x - 1)[d // 2], (0, c_y - 1)[d % 2]
        vc[d] = (-0.25 * zp[x + 1, y + 1]).astype(BF16)

    off_ref[...] = jnp.zeros(off_ref.shape, jnp.int32)
    for far in range(1, n_y):

        def earlier(far=far):
            to_peer(far).wait_recv()
            off_ref[...] += cr[far]

        guarded(iy >= far, earlier)

    def rest_x(d):
        @pl.when(origin_of(d))
        def _():
            for chunk in range(2):
                by_relay(d ^ 1, 1, chunk).wait_recv()

        @pl.when(jnp.logical_not(origin_of(d)))
        def _():
            from_face(d, 1).wait_recv()

    half = c_y // 2
    for d in range(4):
        guarded(diagonals[d][0], lambda d=d: from_corner(d).wait_recv())
    for d in (0, 1):
        guarded(faces[d][0], lambda d=d: from_face(d, 0).wait_recv())
    corner_ref[0, 0] = along_lanes([row_dot(vc[d], rc[d]) for d in range(4)])
    products = [block_dot(vx.at[d], 0, rx.at[d], 0, half) for d in range(2)]
    face_ref[0, 0, :, 0 : 2 * rows] = along_lanes(products)
    for d in (2, 3):
        guarded(faces[d][0], lambda d=d: from_face(d, 0).wait_recv())
    for d in (0, 1):
        guarded(faces[d][0], lambda d=d: rest_x(d))
    products = [block_dot(vx.at[d], half, rx.at[d], half, half) for d in range(2)]
    face_ref[0, 0, :, 0 : 2 * rows] += along_lanes(products)
    products = [block_dot(vy.at[d], 0, ry.at[d], 0, c_x) for d in range(2)]
    face_ref[0, 0, :, 2 * rows : 4 * rows] = along_lanes(products)

    def sent(d):
        to_face(d, 0).wait_send()
        if d < 2:

            @pl.when(origin_of(d))
            def _():
                for chunk in range(2):
                    by_relay(d, 0, chunk).wait_send()

            @pl.when(jnp.logical_not(origin_of(d)))
            def _():
                to_face(d, 1).wait_send()

    for d in range(4):
        guarded(faces[d][0], lambda d=d: sent(d))
        guarded(diagonals[d][0], lambda d=d: to_corner(d).wait_send())

    @pl.when(is_relay)
    def _():
        for chunk in range(2):
            by_relay(0, 1, chunk).wait_send()

    for far in range(1, n_y):
        guarded(iy + far < n_y, lambda far=far: to_peer(far).wait_send())


def hand_on(own_in, face_in, corner_in, off_in, own_out, face_out, corner_out, off_out, wide, first, sems):
    pairs = [(off_in, wide), (face_in, face_out), (corner_in, corner_out), (own_in, own_out)]
    copies = [pltpu.make_async_copy(a, b, sems.at[i]) for i, (a, b) in enumerate(pairs)]
    for copy in copies:
        copy.start()
    copies[0].wait()
    first[...] = wide[0:1, 0:1]
    last = pltpu.make_async_copy(first, off_out, sems.at[len(pairs)])
    last.start()
    for copy in copies[1:]:
        copy.wait()
    last.wait()


def on_device(n_x, n_y, vectors, root_stiff, diag_coef, counts):
    rows, c_x, c_y, c_z = vectors.shape
    vmem = pltpu.VMEM
    results = (
        jax.ShapeDtypeStruct((1, 1, rows, rows), F32),
        jax.ShapeDtypeStruct((1, 1, rows, 4 * rows), F32),
        jax.ShapeDtypeStruct((1, 1, rows, 4 * rows), F32),
        jax.ShapeDtypeStruct((1, 1), jnp.int32),
    )
    anywhere = pl.BlockSpec(memory_space=pl.ANY)
    outputs = pl.pallas_call(
        functools.partial(kernel, n_x, n_y),
        out_shape=results[:3] + (jax.ShapeDtypeStruct((8, c_z), jnp.int32),),
        in_specs=[anywhere] * 3 + [pl.BlockSpec(memory_space=pltpu.SMEM)],
        out_specs=[pl.BlockSpec(memory_space=vmem)] * 4,
        scratch_shapes=[
            vmem((c_x, rows, c_y, c_z), BF16),
            vmem((c_x, c_y, c_z), F32),
            vmem((c_x, c_y, c_z), F32),
            vmem((c_x, rows * (c_y + 1) + 7, c_z), F32),
            vmem((c_x, c_y, rows, c_z), BF16),
            vmem((2, c_y, rows, c_z), BF16),
            vmem((c_x, rows, c_z), BF16),
            vmem((c_x, rows, c_z), BF16),
            vmem((c_x + 2, c_y + 2, rows, c_z), F32),
            vmem((2, c_y, rows, c_z), BF16),
            vmem((2, c_y, rows, c_z), BF16),
            vmem((2, c_x, rows, c_z), BF16),
            vmem((2, c_y, rows, c_z), BF16),
            vmem((2, c_x, rows, c_z), BF16),
            vmem((4, rows, c_z), BF16),
            vmem((2, c_y // 4, rows, c_z), BF16),
            vmem((4, rows, c_z), BF16),
            vmem((8, c_z), jnp.int32),
            vmem((n_y, 8, c_z), jnp.int32),
            pltpu.SemaphoreType.DMA((c_x + 2,)),
            pltpu.SemaphoreType.DMA((12,)),
            pltpu.SemaphoreType.DMA((12,)),
            pltpu.SemaphoreType.DMA((n_y,)),
            pltpu.SemaphoreType.DMA((n_y,)),
            pltpu.SemaphoreType.DMA((2, 2, 2)),
        ],
        compiler_params=pltpu.CompilerParams(
            collective_id=0, has_side_effects=True, vmem_limit_bytes=55040 * 1024
        ),
        cost_estimate=pl.CostEstimate(flops=600_000_000, bytes_accessed=5_000_000, transcendentals=0),
        name="coarse",
    )(vectors, root_stiff, diag_coef, counts)
    return pl.pallas_call(
        hand_on,
        out_shape=results,
        in_specs=[anywhere] * 4,
        out_specs=[anywhere] * 4,
        scratch_shapes=[
            vmem((8, c_z), jnp.int32),
            vmem((1, 1), jnp.int32),
            pltpu.SemaphoreType.DMA((5,)),
        ],
        name="results",
        compiler_params=pltpu.CompilerParams(vmem_limit_bytes=4 * 1024 * 1024),
    )(*outputs)


def solution(mesh):
    n_x, n_y = mesh.shape["sx"], mesh.shape["sy"]
    return jax.shard_map(
        functools.partial(on_device, n_x, n_y),
        mesh=mesh,
        in_specs=(
            P(None, "sx", "sy", None),
            P("sx", "sy", None),
            P("sx", "sy", None),
            P("sx", "sy"),
        ),
        out_specs=(
            P("sx", "sy", None, None),
            P("sx", "sy", None, None),
            P("sx", "sy", None, None),
            P("sx", "sy"),
        ),
        check_vma=False,
    )
```

```python
import functools

import jax
import jax.numpy as jnp
from jax import lax
from jax.experimental import pallas as pl
from jax.experimental.pallas import tpu as pltpu
from jax.sharding import PartitionSpec as P

MESH = pl.DeviceIdType.MESH
F32 = jnp.float32
BF16 = jnp.bfloat16
SHARE = 16


def row_dot(left, right):
    return lax.dot_general(left, right, (((1,), (1,)), ((), ())), preferred_element_type=F32)


def along_lanes(pieces):
    return jnp.concatenate(pieces, axis=1)


def block_dot(left_ref, left_start, right_ref, right_start, count):
    return row_dot(
        along_lanes([left_ref[left_start + i] for i in range(count)]),
        along_lanes([right_ref[right_start + i] for i in range(count)]),
    )


def kernel(
    n_x,
    n_y,
    vec_ref,
    rs_ref,
    dg_ref,
    cnt_ref,
    own_ref,
    face_ref,
    corner_ref,
    off_ref,
    vv,
    rs,
    dg,
    wide,
    mb,
    sx,
    sy,
    zp,
    ab,
    vx,
    vy,
    rx,
    ry,
    rc,
    rr,
    vc,
    cb,
    cr,
    load_sem,
    send_sem,
    recv_sem,
    csend_sem,
    crecv_sem,
    relay_sem,
    across_sem,
):
    rows, c_x, c_y, c_z = vec_ref.shape
    direct = c_y * SHARE // 32
    chunk_rows = (c_y - direct) // 2
    pitch = c_y + 1
    ix, iy = lax.axis_index("sx"), lax.axis_index("sy")

    def guarded(there, action):
        @pl.when(there)
        def _():
            action()

    low_x, high_x = ix > 0, ix < n_x - 1
    low_y, high_y = iy > 0, iy < n_y - 1
    faces = [
        (low_x, (ix - 1, iy)),
        (high_x, (ix + 1, iy)),
        (low_y, (ix, iy - 1)),
        (high_y, (ix, iy + 1)),
    ]
    across_low, across_high = n_x // 2 - 1, n_x // 2

    def at_once(d):
        return (ix == (across_high, across_low)[d]) | (ix == (n_x - 2, n_x - 3)[d])

    def place(x):
        return (0, *range(2, c_x), 1)[x]

    def origin_of(d):
        return ix == (across_high, across_low)[d]

    def across(d, side):
        return faces[d][1][0], iy - 1 + 2 * side

    barrier = pltpu.get_barrier_semaphore()
    for there, device in faces:

        @pl.when(there)
        def _(device=device):
            pl.semaphore_signal(barrier, inc=1, device_id=device, device_id_type=MESH)

    for far in range(2, n_y):

        @pl.when(iy >= far)
        def _(far=far):
            pl.semaphore_signal(barrier, inc=1, device_id=(ix, iy - far), device_id_type=MESH)

    is_origin = (ix == across_low) | (ix == across_high)
    is_relay = (ix == 0) | (ix == n_x - 1)
    via_y = iy + 1 - 2 * lax.rem(iy, 2)
    origin_to = (jnp.where(ix == across_low, n_x - 1, 0), via_y)
    relay_to = (jnp.where(ix == 0, across_low, across_high), via_y)
    relay_from = (jnp.where(ix == 0, across_high, across_low), via_y)
    target_from = (jnp.where(ix == across_low, 0, n_x - 1), via_y)

    @pl.when(is_relay)
    def _():
        pl.semaphore_signal(barrier, inc=1, device_id=relay_from, device_id_type=MESH)

    @pl.when(is_origin)
    def _():
        pl.semaphore_signal(barrier, inc=1, device_id=target_from, device_id_type=MESH)

    def load(x):
        return pltpu.make_async_copy(vec_ref.at[:, x], vv.at[x], load_sem.at[x])

    rs_load = pltpu.make_async_copy(rs_ref, rs, load_sem.at[c_x])
    dg_load = pltpu.make_async_copy(dg_ref, dg, load_sem.at[c_x + 1])
    rs_load.start()
    load(0).start()
    load(c_x - 1).start()
    for x in range(1, c_x - 1):
        load(x).start()
    dg_load.start()

    greeted = sum(there.astype(jnp.int32) for there, _ in faces)
    greeted = greeted + (is_relay | is_origin).astype(jnp.int32)
    for side, there in enumerate((low_y, high_y)):
        for d in range(2):

            @pl.when(at_once(d) & there)
            def _(side=side, d=d):
                pl.semaphore_signal(barrier, inc=1, device_id=across(d, side), device_id_type=MESH)

        greeted = greeted + ((at_once(0) | at_once(1)) & there).astype(jnp.int32)
    greeted = greeted + jnp.maximum(n_y - 2 - iy, 0)

    def zero_layers(ref):
        def step(i, _):
            ref[i] = jnp.zeros((rows, c_z), BF16)
            return _

        lax.fori_loop(0, ref.shape[0], step, 0)

    for d in range(4):
        layers = rx.at[d] if d < 2 else ry.at[d - 2]
        guarded(jnp.logical_not(faces[d][0]), lambda layers=layers: zero_layers(layers))

        if d < 2:

            @pl.when(jnp.logical_not(faces[d][0]))
            def _(d=d):
                rc[2 * d] = jnp.zeros((rows, c_z), BF16)
                rc[2 * d + 1] = jnp.zeros((rows, c_z), BF16)

            for side, there in enumerate((low_y, high_y)):

                @pl.when(at_once(d) & jnp.logical_not(there))
                def _(d=d, side=side):
                    rc[2 * d + side] = jnp.zeros((rows, c_z), BF16)

    lane_r = lax.broadcasted_iota(jnp.int32, (c_z, c_z), 0)
    lane_c = lax.broadcasted_iota(jnp.int32, (c_z, c_z), 1)
    apart = jnp.abs(lane_r - lane_c)
    smooth = jnp.where(apart == 0, 1.0, jnp.where(apart == 1, 0.5, 0.0)).astype(BF16)

    def zero_row(y, _):
        zp[0, y] = jnp.zeros((rows, c_z), F32)
        zp[c_x + 1, y] = jnp.zeros((rows, c_z), F32)
        return _

    lax.fori_loop(0, c_y + 2, zero_row, 0)
    for x in range(1, c_x + 1):
        zp[x, 0] = jnp.zeros((rows, c_z), F32)
        zp[x, c_y + 1] = jnp.zeros((rows, c_z), F32)

    count = cnt_ref[0, 0]
    cb[...] = jnp.full(cb.shape, count, jnp.int32)
    keep = lax.broadcasted_iota(jnp.int32, (rows, c_z), 0) < count

    def widen(x):
        load(x).wait()
        for a in range(rows):
            wide[x, a * pitch : a * pitch + c_y, :] = vv[x, a].astype(F32)

    def row(x, y):
        m = jnp.where(keep, wide[x, pl.ds(y, rows, stride=pitch), :], 0.0)
        return m, m * rs[x, y : y + 1, :]

    def smoothed(x, pieces):
        z = jnp.dot(jnp.concatenate(pieces, axis=0), smooth, preferred_element_type=F32)
        for y in range(c_y):
            zp[x + 1, y + 1] = z[y * rows : (y + 1) * rows]

    def scale(x):
        pieces = []
        for y in range(c_y):
            m, s = row(x, y)
            mb[x, y] = m.astype(BF16)
            pieces.append(s.astype(BF16))
        smoothed(x, pieces)

    rs_load.wait()
    for side, x in enumerate((0, c_x - 1)):
        widen(x)
        for y in range(c_y):
            m, s = row(x, y)
            mb[x, y] = m.astype(BF16)
            sx[side, y] = s.astype(BF16)

    def widen_step(x, _):
        widen(x)
        return _

    lax.fori_loop(1, c_x - 1, widen_step, 0)
    for x in range(c_x):
        sy[0, place(x)] = row(x, 0)[1].astype(BF16)
        sy[1, place(x)] = row(x, c_y - 1)[1].astype(BF16)

    pl.semaphore_wait(barrier, greeted)

    def to_face(d, part, to=None):
        opposite = d ^ 1
        if d < 2:
            piece = pl.ds(direct, c_y - direct) if part else pl.ds(0, direct)
            src, dst = sx.at[d, piece], rx.at[opposite, piece]
        else:
            piece = pl.ds(2, c_x - 2) if part else pl.ds(0, 2)
            src, dst = sy.at[d - 2, piece], ry.at[opposite - 2, piece]
        return pltpu.make_async_remote_copy(
            src_ref=src,
            dst_ref=dst,
            send_sem=send_sem.at[part * 4 + d],
            recv_sem=recv_sem.at[part * 4 + opposite],
            device_id=faces[d if to is None else to][1],
            device_id_type=MESH,
        )

    def from_face(d, part):
        return to_face(d ^ 1, part, d)

    def by_relay(d, leg, chunk):
        opposite = d ^ 1
        piece = pl.ds(direct + chunk * chunk_rows, chunk_rows)
        src, dst = [
            (sx.at[d, piece], rr.at[chunk]),
            (rr.at[chunk], rx.at[opposite, piece]),
        ][leg]
        return pltpu.make_async_remote_copy(
            src_ref=src,
            dst_ref=dst,
            send_sem=relay_sem.at[0, leg, chunk],
            recv_sem=relay_sem.at[1, leg, chunk],
            device_id=(origin_to, relay_to)[leg],
            device_id_type=MESH,
        )

    def to_corner(d, to=None):
        opposite = d ^ 1
        return pltpu.make_async_remote_copy(
            src_ref=ry.at[pl.ds(0, 2), d],
            dst_ref=rc.at[pl.ds(2 * opposite, 2)],
            send_sem=send_sem.at[8 + d],
            recv_sem=recv_sem.at[8 + opposite],
            device_id=faces[d if to is None else to][1],
            device_id_type=MESH,
        )

    def to_across(d, side, device=None):
        return pltpu.make_async_remote_copy(
            src_ref=sy.at[side, d],
            dst_ref=rc.at[2 * (d ^ 1) + 1 - side],
            send_sem=across_sem.at[0, side],
            recv_sem=across_sem.at[1, 1 - side],
            device_id=across(d, side) if device is None else device,
            device_id_type=MESH,
        )

    def from_across(d, side):
        return to_across(d ^ 1, 1 - side, across(d, side))

    def at_across(action):
        for side, there in enumerate((low_y, high_y)):
            for d in range(2):
                guarded(at_once(d) & there, lambda side=side, d=d: action(d, side))

    def from_corner(d):
        return to_corner(d ^ 1, d)

    def to_peer(far):
        return pltpu.make_async_remote_copy(
            src_ref=cb,
            dst_ref=cr.at[far],
            send_sem=csend_sem.at[far],
            recv_sem=crecv_sem.at[far],
            device_id=(ix, iy + far),
            device_id_type=MESH,
        )

    def onward(d):
        return faces[d][0] & jnp.logical_not(at_once(d))

    def send_x(d):
        @pl.when(origin_of(d))
        def _():
            for chunk in range(2):
                by_relay(d, 0, chunk).start()

        to_face(d, 0).start()

        @pl.when(jnp.logical_not(origin_of(d)))
        def _():
            to_face(d, 1).start()

    for d in (3, 2):
        guarded(faces[d][0], lambda d=d: to_face(d, 0).start())
    at_across(lambda d, side: to_across(d, side).start())
    for d in (1, 0):
        guarded(faces[d][0], lambda d=d: send_x(d))
    for d in (3, 2):
        guarded(faces[d][0], lambda d=d: to_face(d, 1).start())
    for far in range(1, n_y):
        guarded(iy + far < n_y, lambda far=far: to_peer(far).start())

    for side, x in enumerate((0, c_x - 1)):
        smoothed(x, [sx[side, y] for y in range(c_y)])

    def scale_step(x, _):
        scale(x)
        return _

    lax.fori_loop(1, c_x - 1, scale_step, 0)

    for side, x in enumerate((1, c_x)):
        for y in range(c_y):
            vx[side, y] = (
                -0.25 * ((zp[x, y] + zp[x, y + 2]) + 2.0 * zp[x, y + 1])
            ).astype(BF16)
    for side, y in enumerate((1, c_y)):
        for x in range(c_x):
            vy[side, place(x)] = (
                -0.25 * ((zp[x, y] + zp[x + 2, y]) + 2.0 * zp[x + 1, y])
            ).astype(BF16)

    dg_load.wait()
    dg[...] = dg[...] + rs[...] * rs[...]
    rs[...] = rs[...] * 0.25

    def apply(x, slot):
        def across(y):
            near = zp[x + 1, y]
            return (zp[x, y] + near) + (near + zp[x + 2, y])

        here = across(1)
        before = here
        for y in range(c_y):
            ahead = across(y + 2)
            after = here + ahead
            m = mb[x, y].astype(F32)
            applied = dg[x, pl.ds(y, 1), :] * m - rs[x, pl.ds(y, 1), :] * (before + after)
            ab[slot, y] = applied.astype(BF16)
            here, before = ahead, after

    def product(x, slot):
        return block_dot(mb.at[x], 0, ab.at[slot], 0, c_y)

    apply(0, 0)

    def own_step(i, total):
        x = 2 * i
        total = total + product(x, 0)
        apply(x + 1, 1)
        total = total + product(x + 1, 1)
        apply(x + 2, 0)
        return total

    def hand_on_corners():
        for d in (2, 3):
            guarded(faces[d][0], lambda d=d: from_face(d, 0).wait_recv())
        for d in (0, 1):
            guarded(onward(d), lambda d=d: to_corner(d).start())

    def hand_over(d, chunk):
        by_relay(d, 0, chunk).wait_recv()
        by_relay(d, 1, chunk).start()

    total = jnp.zeros((rows, rows), F32)
    for step in range(c_x // 2 - 1):
        total = lax.fori_loop(step, step + 1, own_step, total)
        if step < 2:
            guarded(ix == 0, lambda step=step: hand_over(0, step))
            guarded(ix == n_x - 1, lambda step=step: hand_over(1, step))
        if step == 1:
            hand_on_corners()
    total = total + product(c_x - 2, 0)
    apply(c_x - 1, 1)
    own_ref[0, 0] = total + product(c_x - 1, 1)

    for d in range(4):
        x, y = (0, c_x - 1)[d // 2], (0, c_y - 1)[d % 2]
        vc[d] = (-0.25 * zp[x + 1, y + 1]).astype(BF16)

    off_ref[...] = jnp.zeros(off_ref.shape, jnp.int32)
    for far in range(1, n_y):

        def earlier(far=far):
            to_peer(far).wait_recv()
            off_ref[...] += cr[far]

        guarded(iy >= far, earlier)

    def rest_x(d):
        @pl.when(origin_of(d))
        def _():
            for chunk in range(2):
                by_relay(d ^ 1, 1, chunk).wait_recv()

        @pl.when(jnp.logical_not(origin_of(d)))
        def _():
            from_face(d, 1).wait_recv()

    for d in (0, 1):
        guarded(onward(d), lambda d=d: from_corner(d).wait_recv())
    at_across(lambda d, side: from_across(d, side).wait_recv())
    for d in (0, 1):
        guarded(faces[d][0], lambda d=d: from_face(d, 0).wait_recv())
    corner_ref[0, 0] = along_lanes([row_dot(vc[d], rc[d]) for d in range(4)])
    products = [block_dot(vx.at[d], 0, rx.at[d], 0, direct) for d in range(2)]
    face_ref[0, 0, :, 0 : 2 * rows] = along_lanes(products)
    for d in (2, 3):
        guarded(faces[d][0], lambda d=d: from_face(d, 1).wait_recv())
    for d in (0, 1):
        guarded(faces[d][0], lambda d=d: rest_x(d))
    products = [block_dot(vx.at[d], direct, rx.at[d], direct, c_y - direct) for d in range(2)]
    face_ref[0, 0, :, 0 : 2 * rows] += along_lanes(products)
    products = [block_dot(vy.at[d], 0, ry.at[d], 0, c_x) for d in range(2)]
    face_ref[0, 0, :, 2 * rows : 4 * rows] = along_lanes(products)

    def sent(d):
        to_face(d, 0).wait_send()
        if d >= 2:
            to_face(d, 1).wait_send()
        else:
            guarded(onward(d), lambda: to_corner(d).wait_send())

            @pl.when(origin_of(d))
            def _():
                for chunk in range(2):
                    by_relay(d, 0, chunk).wait_send()

            @pl.when(jnp.logical_not(origin_of(d)))
            def _():
                to_face(d, 1).wait_send()

    for d in range(4):
        guarded(faces[d][0], lambda d=d: sent(d))
    at_across(lambda d, side: to_across(d, side).wait_send())

    @pl.when(is_relay)
    def _():
        for chunk in range(2):
            by_relay(0, 1, chunk).wait_send()

    for far in range(1, n_y):
        guarded(iy + far < n_y, lambda far=far: to_peer(far).wait_send())


def hand_on(own_in, face_in, corner_in, off_in, own_out, face_out, corner_out, off_out, wide, first, sems):
    pairs = [(off_in, wide), (face_in, face_out), (corner_in, corner_out), (own_in, own_out)]
    copies = [pltpu.make_async_copy(a, b, sems.at[i]) for i, (a, b) in enumerate(pairs)]
    for copy in copies:
        copy.start()
    copies[0].wait()
    first[...] = wide[0:1, 0:1]
    last = pltpu.make_async_copy(first, off_out, sems.at[len(pairs)])
    last.start()
    for copy in copies[1:]:
        copy.wait()
    last.wait()


def on_device(n_x, n_y, vectors, root_stiff, diag_coef, counts):
    rows, c_x, c_y, c_z = vectors.shape
    vmem = pltpu.VMEM
    results = (
        jax.ShapeDtypeStruct((1, 1, rows, rows), F32),
        jax.ShapeDtypeStruct((1, 1, rows, 4 * rows), F32),
        jax.ShapeDtypeStruct((1, 1, rows, 4 * rows), F32),
        jax.ShapeDtypeStruct((1, 1), jnp.int32),
    )
    anywhere = pl.BlockSpec(memory_space=pl.ANY)
    outputs = pl.pallas_call(
        functools.partial(kernel, n_x, n_y),
        out_shape=results[:3] + (jax.ShapeDtypeStruct((8, c_z), jnp.int32),),
        in_specs=[anywhere] * 3 + [pl.BlockSpec(memory_space=pltpu.SMEM)],
        out_specs=[pl.BlockSpec(memory_space=vmem)] * 4,
        scratch_shapes=[
            vmem((c_x, rows, c_y, c_z), BF16),
            vmem((c_x, c_y, c_z), F32),
            vmem((c_x, c_y, c_z), F32),
            vmem((c_x, rows * (c_y + 1) + 7, c_z), F32),
            vmem((c_x, c_y, rows, c_z), BF16),
            vmem((2, c_y, rows, c_z), BF16),
            vmem((2, c_x, rows, c_z), BF16),
            vmem((c_x + 2, c_y + 2, rows, c_z), F32),
            vmem((2, c_y, rows, c_z), BF16),
            vmem((2, c_y, rows, c_z), BF16),
            vmem((2, c_x, rows, c_z), BF16),
            vmem((2, c_y, rows, c_z), BF16),
            vmem((2, c_x, rows, c_z), BF16),
            vmem((4, rows, c_z), BF16),
            vmem((2, (c_y - c_y * SHARE // 32) // 2, rows, c_z), BF16),
            vmem((4, rows, c_z), BF16),
            vmem((8, c_z), jnp.int32),
            vmem((n_y, 8, c_z), jnp.int32),
            pltpu.SemaphoreType.DMA((c_x + 2,)),
            pltpu.SemaphoreType.DMA((12,)),
            pltpu.SemaphoreType.DMA((12,)),
            pltpu.SemaphoreType.DMA((n_y,)),
            pltpu.SemaphoreType.DMA((n_y,)),
            pltpu.SemaphoreType.DMA((2, 2, 2)),
            pltpu.SemaphoreType.DMA((2, 2)),
        ],
        compiler_params=pltpu.CompilerParams(
            collective_id=0, has_side_effects=True, vmem_limit_bytes=55040 * 1024
        ),
        cost_estimate=pl.CostEstimate(flops=600_000_000, bytes_accessed=5_000_000, transcendentals=0),
        name="coarse",
    )(vectors, root_stiff, diag_coef, counts)
    return pl.pallas_call(
        hand_on,
        out_shape=results,
        in_specs=[anywhere] * 4,
        out_specs=[anywhere] * 4,
        scratch_shapes=[
            vmem((8, c_z), jnp.int32),
            vmem((1, 1), jnp.int32),
            pltpu.SemaphoreType.DMA((5,)),
        ],
        name="results",
        compiler_params=pltpu.CompilerParams(vmem_limit_bytes=4 * 1024 * 1024),
    )(*outputs)


def solution(mesh):
    n_x, n_y = mesh.shape["sx"], mesh.shape["sy"]
    return jax.shard_map(
        functools.partial(on_device, n_x, n_y),
        mesh=mesh,
        in_specs=(
            P(None, "sx", "sy", None),
            P("sx", "sy", None),
            P("sx", "sy", None),
            P("sx", "sy"),
        ),
        out_specs=(
            P("sx", "sy", None, None),
            P("sx", "sy", None, None),
            P("sx", "sy", None, None),
            P("sx", "sy"),
        ),
        check_vma=False,
    )
```

```python
import functools

import jax
import jax.numpy as jnp
from jax import lax
from jax.experimental import pallas as pl
from jax.experimental.pallas import tpu as pltpu
from jax.sharding import PartitionSpec as P

MESH = pl.DeviceIdType.MESH
F32 = jnp.float32
BF16 = jnp.bfloat16
SHARE = 16


def row_dot(left, right):
    return lax.dot_general(left, right, (((1,), (1,)), ((), ())), preferred_element_type=F32)


def along_lanes(pieces):
    return jnp.concatenate(pieces, axis=1)


def block_dot(left_ref, left_start, right_ref, right_start, count):
    return row_dot(
        along_lanes([left_ref[left_start + i] for i in range(count)]),
        along_lanes([right_ref[right_start + i] for i in range(count)]),
    )


def kernel(
    n_x,
    n_y,
    vec_ref,
    rs_ref,
    dg_ref,
    cnt_ref,
    own_ref,
    face_ref,
    corner_ref,
    off_ref,
    vv,
    rs,
    dg,
    wide,
    mb,
    sx,
    sy,
    zp,
    ab,
    vx,
    vy,
    rx,
    ry,
    rc,
    rr,
    vc,
    cb,
    cr,
    load_sem,
    send_sem,
    recv_sem,
    csend_sem,
    crecv_sem,
    relay_sem,
    across_sem,
    sum_out,
    sum_in,
    tell_sem,
):
    rows, c_x, c_y, c_z = vec_ref.shape
    direct = c_y * SHARE // 32
    chunk_rows = (c_y - direct) // 2
    pitch = c_y + 1
    ix, iy = lax.axis_index("sx"), lax.axis_index("sy")

    def guarded(there, action):
        @pl.when(there)
        def _():
            action()

    low_x, high_x = ix > 0, ix < n_x - 1
    low_y, high_y = iy > 0, iy < n_y - 1
    faces = [
        (low_x, (ix - 1, iy)),
        (high_x, (ix + 1, iy)),
        (low_y, (ix, iy - 1)),
        (high_y, (ix, iy + 1)),
    ]
    across_low, across_high = n_x // 2 - 1, n_x // 2

    def at_once(d):
        return (ix == (across_high, across_low)[d]) | (ix == (n_x - 2, n_x - 3)[d])

    def place(x):
        return (0, *range(2, c_x), 1)[x]

    def origin_of(d):
        return ix == (across_high, across_low)[d]

    def across(d, side):
        return faces[d][1][0], iy - 1 + 2 * side

    barrier = pltpu.get_barrier_semaphore()
    for there, device in faces:

        @pl.when(there)
        def _(device=device):
            pl.semaphore_signal(barrier, inc=1, device_id=device, device_id_type=MESH)

    mid = n_y // 2
    upper = iy >= mid
    slot = lax.rem(iy, mid)
    is_teller = iy == mid - 1
    for far in range(2, mid):

        @pl.when(slot >= far)
        def _(far=far):
            pl.semaphore_signal(barrier, inc=1, device_id=(ix, iy - far), device_id_type=MESH)

    @pl.when(iy > mid)
    def _():
        pl.semaphore_signal(barrier, inc=1, device_id=(ix, mid - 1), device_id_type=MESH)

    is_origin = (ix == across_low) | (ix == across_high)
    is_relay = (ix == 0) | (ix == n_x - 1)
    via_y = iy + 1 - 2 * lax.rem(iy, 2)
    origin_to = (jnp.where(ix == across_low, n_x - 1, 0), via_y)
    relay_to = (jnp.where(ix == 0, across_low, across_high), via_y)
    relay_from = (jnp.where(ix == 0, across_high, across_low), via_y)
    target_from = (jnp.where(ix == across_low, 0, n_x - 1), via_y)

    @pl.when(is_relay)
    def _():
        pl.semaphore_signal(barrier, inc=1, device_id=relay_from, device_id_type=MESH)

    @pl.when(is_origin)
    def _():
        pl.semaphore_signal(barrier, inc=1, device_id=target_from, device_id_type=MESH)

    def load(x):
        return pltpu.make_async_copy(vec_ref.at[:, x], vv.at[x], load_sem.at[x])

    rs_load = pltpu.make_async_copy(rs_ref, rs, load_sem.at[c_x])
    dg_load = pltpu.make_async_copy(dg_ref, dg, load_sem.at[c_x + 1])
    rs_load.start()
    load(0).start()
    load(c_x - 1).start()
    for x in range(1, c_x - 1):
        load(x).start()
    dg_load.start()

    greeted = sum(there.astype(jnp.int32) for there, _ in faces)
    greeted = greeted + (is_relay | is_origin).astype(jnp.int32)
    for side, there in enumerate((low_y, high_y)):
        for d in range(2):

            @pl.when(at_once(d) & there)
            def _(side=side, d=d):
                pl.semaphore_signal(barrier, inc=1, device_id=across(d, side), device_id_type=MESH)

        greeted = greeted + ((at_once(0) | at_once(1)) & there).astype(jnp.int32)
    greeted = greeted + jnp.maximum(mid - 2 - slot, 0)
    greeted = greeted + jnp.where(is_teller, n_y - mid - 1, 0)

    def zero_layers(ref):
        def step(i, _):
            ref[i] = jnp.zeros((rows, c_z), BF16)
            return _

        lax.fori_loop(0, ref.shape[0], step, 0)

    for d in range(4):
        layers = rx.at[d] if d < 2 else ry.at[d - 2]
        guarded(jnp.logical_not(faces[d][0]), lambda layers=layers: zero_layers(layers))

        if d < 2:

            @pl.when(jnp.logical_not(faces[d][0]))
            def _(d=d):
                rc[2 * d] = jnp.zeros((rows, c_z), BF16)
                rc[2 * d + 1] = jnp.zeros((rows, c_z), BF16)

            for side, there in enumerate((low_y, high_y)):

                @pl.when(at_once(d) & jnp.logical_not(there))
                def _(d=d, side=side):
                    rc[2 * d + side] = jnp.zeros((rows, c_z), BF16)

    lane_r = lax.broadcasted_iota(jnp.int32, (c_z, c_z), 0)
    lane_c = lax.broadcasted_iota(jnp.int32, (c_z, c_z), 1)
    apart = jnp.abs(lane_r - lane_c)
    smooth = jnp.where(apart == 0, 1.0, jnp.where(apart == 1, 0.5, 0.0)).astype(BF16)

    def zero_row(y, _):
        zp[0, y] = jnp.zeros((rows, c_z), F32)
        zp[c_x + 1, y] = jnp.zeros((rows, c_z), F32)
        return _

    lax.fori_loop(0, c_y + 2, zero_row, 0)
    for x in range(1, c_x + 1):
        zp[x, 0] = jnp.zeros((rows, c_z), F32)
        zp[x, c_y + 1] = jnp.zeros((rows, c_z), F32)

    count = cnt_ref[0, 0]
    cb[...] = jnp.full(cb.shape, count, jnp.int32)
    keep = lax.broadcasted_iota(jnp.int32, (rows, c_z), 0) < count

    def widen(x):
        load(x).wait()
        for a in range(rows):
            wide[x, a * pitch : a * pitch + c_y, :] = vv[x, a].astype(F32)

    def row(x, y):
        m = jnp.where(keep, wide[x, pl.ds(y, rows, stride=pitch), :], 0.0)
        return m, m * rs[x, y : y + 1, :]

    def smoothed(x, pieces):
        z = jnp.dot(jnp.concatenate(pieces, axis=0), smooth, preferred_element_type=F32)
        for y in range(c_y):
            zp[x + 1, y + 1] = z[y * rows : (y + 1) * rows]

    def scale(x):
        pieces = []
        for y in range(c_y):
            m, s = row(x, y)
            mb[x, y] = m.astype(BF16)
            pieces.append(s.astype(BF16))
        smoothed(x, pieces)

    rs_load.wait()
    for side, x in enumerate((0, c_x - 1)):
        widen(x)
        for y in range(c_y):
            m, s = row(x, y)
            mb[x, y] = m.astype(BF16)
            sx[side, y] = s.astype(BF16)

    def widen_step(x, _):
        widen(x)
        return _

    lax.fori_loop(1, c_x - 1, widen_step, 0)
    for x in range(c_x):
        sy[0, place(x)] = row(x, 0)[1].astype(BF16)
        sy[1, place(x)] = row(x, c_y - 1)[1].astype(BF16)

    pl.semaphore_wait(barrier, greeted)

    def to_face(d, part, to=None):
        opposite = d ^ 1
        if d < 2:
            piece = pl.ds(direct, c_y - direct) if part else pl.ds(0, direct)
            src, dst = sx.at[d, piece], rx.at[opposite, piece]
        else:
            piece = pl.ds(2, c_x - 2) if part else pl.ds(0, 2)
            src, dst = sy.at[d - 2, piece], ry.at[opposite - 2, piece]
        return pltpu.make_async_remote_copy(
            src_ref=src,
            dst_ref=dst,
            send_sem=send_sem.at[part * 4 + d],
            recv_sem=recv_sem.at[part * 4 + opposite],
            device_id=faces[d if to is None else to][1],
            device_id_type=MESH,
        )

    def from_face(d, part):
        return to_face(d ^ 1, part, d)

    def by_relay(d, leg, chunk):
        opposite = d ^ 1
        piece = pl.ds(direct + chunk * chunk_rows, chunk_rows)
        src, dst = [
            (sx.at[d, piece], rr.at[chunk]),
            (rr.at[chunk], rx.at[opposite, piece]),
        ][leg]
        return pltpu.make_async_remote_copy(
            src_ref=src,
            dst_ref=dst,
            send_sem=relay_sem.at[0, leg, chunk],
            recv_sem=relay_sem.at[1, leg, chunk],
            device_id=(origin_to, relay_to)[leg],
            device_id_type=MESH,
        )

    def to_corner(d, to=None):
        opposite = d ^ 1
        return pltpu.make_async_remote_copy(
            src_ref=ry.at[pl.ds(0, 2), d],
            dst_ref=rc.at[pl.ds(2 * opposite, 2)],
            send_sem=send_sem.at[8 + d],
            recv_sem=recv_sem.at[8 + opposite],
            device_id=faces[d if to is None else to][1],
            device_id_type=MESH,
        )

    def to_across(d, side, device=None):
        return pltpu.make_async_remote_copy(
            src_ref=sy.at[side, d],
            dst_ref=rc.at[2 * (d ^ 1) + 1 - side],
            send_sem=across_sem.at[0, side],
            recv_sem=across_sem.at[1, 1 - side],
            device_id=across(d, side) if device is None else device,
            device_id_type=MESH,
        )

    def from_across(d, side):
        return to_across(d ^ 1, 1 - side, across(d, side))

    def at_across(action):
        for side, there in enumerate((low_y, high_y)):
            for d in range(2):
                guarded(at_once(d) & there, lambda side=side, d=d: action(d, side))

    def from_corner(d):
        return to_corner(d ^ 1, d)

    def to_peer(far):
        return pltpu.make_async_remote_copy(
            src_ref=cb,
            dst_ref=cr.at[far],
            send_sem=csend_sem.at[far],
            recv_sem=crecv_sem.at[far],
            device_id=(ix, iy + far),
            device_id_type=MESH,
        )

    def onward(d):
        return faces[d][0] & jnp.logical_not(at_once(d))

    def send_x(d):
        @pl.when(origin_of(d))
        def _():
            for chunk in range(2):
                by_relay(d, 0, chunk).start()

        to_face(d, 0).start()

        @pl.when(jnp.logical_not(origin_of(d)))
        def _():
            to_face(d, 1).start()

    for far in range(1, mid):
        guarded(slot + far < mid, lambda far=far: to_peer(far).start())
    for d in (3, 2):
        guarded(faces[d][0], lambda d=d: to_face(d, 0).start())
    at_across(lambda d, side: to_across(d, side).start())
    for d in (1, 0):
        guarded(faces[d][0], lambda d=d: send_x(d))
    for d in (3, 2):
        guarded(faces[d][0], lambda d=d: to_face(d, 1).start())

    for side, x in enumerate((0, c_x - 1)):
        smoothed(x, [sx[side, y] for y in range(c_y)])

    def scale_step(x, _):
        scale(x)
        return _

    lax.fori_loop(1, c_x - 1, scale_step, 0)

    for side, x in enumerate((1, c_x)):
        for y in range(c_y):
            vx[side, y] = (
                -0.25 * ((zp[x, y] + zp[x, y + 2]) + 2.0 * zp[x, y + 1])
            ).astype(BF16)
    for side, y in enumerate((1, c_y)):
        for x in range(c_x):
            vy[side, place(x)] = (
                -0.25 * ((zp[x, y] + zp[x + 2, y]) + 2.0 * zp[x + 1, y])
            ).astype(BF16)

    dg_load.wait()
    dg[...] = dg[...] + rs[...] * rs[...]
    rs[...] = rs[...] * 0.25

    def apply(x, slot):
        def across(y):
            near = zp[x + 1, y]
            return (zp[x, y] + near) + (near + zp[x + 2, y])

        here = across(1)
        before = here
        for y in range(c_y):
            ahead = across(y + 2)
            after = here + ahead
            m = mb[x, y].astype(F32)
            applied = dg[x, pl.ds(y, 1), :] * m - rs[x, pl.ds(y, 1), :] * (before + after)
            ab[slot, y] = applied.astype(BF16)
            here, before = ahead, after

    def product(x, slot):
        return block_dot(mb.at[x], 0, ab.at[slot], 0, c_y)

    apply(0, 0)

    def own_step(i, total):
        x = 2 * i
        total = total + product(x, 0)
        apply(x + 1, 1)
        total = total + product(x + 1, 1)
        apply(x + 2, 0)
        return total

    def to_upper(other):
        return pltpu.make_async_remote_copy(
            src_ref=sum_out,
            dst_ref=sum_in,
            send_sem=tell_sem.at[other - mid],
            recv_sem=tell_sem.at[n_y - mid],
            device_id=(ix, other),
            device_id_type=MESH,
        )

    def add_counts():
        off_ref[...] = jnp.zeros(off_ref.shape, jnp.int32)
        for far in range(1, mid):

            def earlier(far=far):
                to_peer(far).wait_recv()
                off_ref[...] += cr[far]

            guarded(slot >= far, earlier)

        @pl.when(is_teller)
        def _():
            sum_out[...] = off_ref[...] + count
            for other in range(mid, n_y):
                to_upper(other).start()

    def hand_on_corners():
        for d in (2, 3):
            guarded(faces[d][0], lambda d=d: from_face(d, 0).wait_recv())
        for d in (0, 1):
            guarded(onward(d), lambda d=d: to_corner(d).start())

    def hand_over(d, chunk):
        by_relay(d, 0, chunk).wait_recv()
        by_relay(d, 1, chunk).start()

    total = jnp.zeros((rows, rows), F32)
    for step in range(c_x // 2 - 1):
        total = lax.fori_loop(step, step + 1, own_step, total)
        if step < 2:
            guarded(ix == 0, lambda step=step: hand_over(0, step))
            guarded(ix == n_x - 1, lambda step=step: hand_over(1, step))
        if step == 1:
            add_counts()
            hand_on_corners()
    total = total + product(c_x - 2, 0)
    apply(c_x - 1, 1)
    own_ref[0, 0] = total + product(c_x - 1, 1)

    for d in range(4):
        x, y = (0, c_x - 1)[d // 2], (0, c_y - 1)[d % 2]
        vc[d] = (-0.25 * zp[x + 1, y + 1]).astype(BF16)

    def rest_x(d):
        @pl.when(origin_of(d))
        def _():
            for chunk in range(2):
                by_relay(d ^ 1, 1, chunk).wait_recv()

        @pl.when(jnp.logical_not(origin_of(d)))
        def _():
            from_face(d, 1).wait_recv()

    for d in (0, 1):
        guarded(onward(d), lambda d=d: from_corner(d).wait_recv())
    at_across(lambda d, side: from_across(d, side).wait_recv())
    for d in (0, 1):
        guarded(faces[d][0], lambda d=d: from_face(d, 0).wait_recv())
    corner_ref[0, 0] = along_lanes([row_dot(vc[d], rc[d]) for d in range(4)])
    products = [block_dot(vx.at[d], 0, rx.at[d], 0, direct) for d in range(2)]
    face_ref[0, 0, :, 0 : 2 * rows] = along_lanes(products)
    for d in (2, 3):
        guarded(faces[d][0], lambda d=d: from_face(d, 1).wait_recv())
    for d in (0, 1):
        guarded(faces[d][0], lambda d=d: rest_x(d))
    products = [block_dot(vx.at[d], direct, rx.at[d], direct, c_y - direct) for d in range(2)]
    face_ref[0, 0, :, 0 : 2 * rows] += along_lanes(products)
    products = [block_dot(vy.at[d], 0, ry.at[d], 0, c_x) for d in range(2)]
    face_ref[0, 0, :, 2 * rows : 4 * rows] = along_lanes(products)

    @pl.when(upper)
    def _():
        to_upper(mid).wait_recv()
        off_ref[...] += sum_in[...]

    def sent(d):
        to_face(d, 0).wait_send()
        if d >= 2:
            to_face(d, 1).wait_send()
        else:
            guarded(onward(d), lambda: to_corner(d).wait_send())

            @pl.when(origin_of(d))
            def _():
                for chunk in range(2):
                    by_relay(d, 0, chunk).wait_send()

            @pl.when(jnp.logical_not(origin_of(d)))
            def _():
                to_face(d, 1).wait_send()

    for d in range(4):
        guarded(faces[d][0], lambda d=d: sent(d))
    at_across(lambda d, side: to_across(d, side).wait_send())

    @pl.when(is_relay)
    def _():
        for chunk in range(2):
            by_relay(0, 1, chunk).wait_send()

    for far in range(1, mid):
        guarded(slot + far < mid, lambda far=far: to_peer(far).wait_send())

    @pl.when(is_teller)
    def _():
        for other in range(mid, n_y):
            to_upper(other).wait_send()


def hand_on(own_in, face_in, corner_in, off_in, own_out, face_out, corner_out, off_out, wide, first, sems):
    pairs = [(off_in, wide), (face_in, face_out), (corner_in, corner_out), (own_in, own_out)]
    copies = [pltpu.make_async_copy(a, b, sems.at[i]) for i, (a, b) in enumerate(pairs)]
    for copy in copies:
        copy.start()
    copies[0].wait()
    first[...] = wide[0:1, 0:1]
    last = pltpu.make_async_copy(first, off_out, sems.at[len(pairs)])
    last.start()
    for copy in copies[1:]:
        copy.wait()
    last.wait()


def on_device(n_x, n_y, vectors, root_stiff, diag_coef, counts):
    rows, c_x, c_y, c_z = vectors.shape
    vmem = pltpu.VMEM
    results = (
        jax.ShapeDtypeStruct((1, 1, rows, rows), F32),
        jax.ShapeDtypeStruct((1, 1, rows, 4 * rows), F32),
        jax.ShapeDtypeStruct((1, 1, rows, 4 * rows), F32),
        jax.ShapeDtypeStruct((1, 1), jnp.int32),
    )
    anywhere = pl.BlockSpec(memory_space=pl.ANY)
    outputs = pl.pallas_call(
        functools.partial(kernel, n_x, n_y),
        out_shape=results[:3] + (jax.ShapeDtypeStruct((8, c_z), jnp.int32),),
        in_specs=[anywhere] * 3 + [pl.BlockSpec(memory_space=pltpu.SMEM)],
        out_specs=[pl.BlockSpec(memory_space=vmem)] * 4,
        scratch_shapes=[
            vmem((c_x, rows, c_y, c_z), BF16),
            vmem((c_x, c_y, c_z), F32),
            vmem((c_x, c_y, c_z), F32),
            vmem((c_x, rows * (c_y + 1) + 7, c_z), F32),
            vmem((c_x, c_y, rows, c_z), BF16),
            vmem((2, c_y, rows, c_z), BF16),
            vmem((2, c_x, rows, c_z), BF16),
            vmem((c_x + 2, c_y + 2, rows, c_z), F32),
            vmem((2, c_y, rows, c_z), BF16),
            vmem((2, c_y, rows, c_z), BF16),
            vmem((2, c_x, rows, c_z), BF16),
            vmem((2, c_y, rows, c_z), BF16),
            vmem((2, c_x, rows, c_z), BF16),
            vmem((4, rows, c_z), BF16),
            vmem((2, (c_y - c_y * SHARE // 32) // 2, rows, c_z), BF16),
            vmem((4, rows, c_z), BF16),
            vmem((8, c_z), jnp.int32),
            vmem((n_y, 8, c_z), jnp.int32),
            pltpu.SemaphoreType.DMA((c_x + 2,)),
            pltpu.SemaphoreType.DMA((12,)),
            pltpu.SemaphoreType.DMA((12,)),
            pltpu.SemaphoreType.DMA((n_y,)),
            pltpu.SemaphoreType.DMA((n_y,)),
            pltpu.SemaphoreType.DMA((2, 2, 2)),
            pltpu.SemaphoreType.DMA((2, 2)),
            vmem((8, c_z), jnp.int32),
            vmem((8, c_z), jnp.int32),
            pltpu.SemaphoreType.DMA((n_y - n_y // 2 + 1,)),
        ],
        compiler_params=pltpu.CompilerParams(
            collective_id=0, has_side_effects=True, vmem_limit_bytes=55040 * 1024
        ),
        cost_estimate=pl.CostEstimate(flops=600_000_000, bytes_accessed=5_000_000, transcendentals=0),
        name="coarse",
    )(vectors, root_stiff, diag_coef, counts)
    return pl.pallas_call(
        hand_on,
        out_shape=results,
        in_specs=[anywhere] * 4,
        out_specs=[anywhere] * 4,
        scratch_shapes=[
            vmem((8, c_z), jnp.int32),
            vmem((1, 1), jnp.int32),
            pltpu.SemaphoreType.DMA((5,)),
        ],
        name="results",
        compiler_params=pltpu.CompilerParams(vmem_limit_bytes=4 * 1024 * 1024),
    )(*outputs)


def solution(mesh):
    n_x, n_y = mesh.shape["sx"], mesh.shape["sy"]
    return jax.shard_map(
        functools.partial(on_device, n_x, n_y),
        mesh=mesh,
        in_specs=(
            P(None, "sx", "sy", None),
            P("sx", "sy", None),
            P("sx", "sy", None),
            P("sx", "sy"),
        ),
        out_specs=(
            P("sx", "sy", None, None),
            P("sx", "sy", None, None),
            P("sx", "sy", None, None),
            P("sx", "sy"),
        ),
        check_vma=False,
    )
```

```python
import functools

import jax
import jax.numpy as jnp
from jax import lax
from jax.experimental import pallas as pl
from jax.experimental.pallas import tpu as pltpu
from jax.sharding import PartitionSpec as P

MESH = pl.DeviceIdType.MESH
F32 = jnp.float32
BF16 = jnp.bfloat16
SHARE = 16


def row_dot(left, right):
    return lax.dot_general(left, right, (((1,), (1,)), ((), ())), preferred_element_type=F32)


def along_lanes(pieces):
    return jnp.concatenate(pieces, axis=1)


def block_dot(left_ref, left_start, right_ref, right_start, count):
    return row_dot(
        along_lanes([left_ref[left_start + i] for i in range(count)]),
        along_lanes([right_ref[right_start + i] for i in range(count)]),
    )


def kernel(
    n_x,
    n_y,
    vec_ref,
    rs_ref,
    dg_ref,
    cnt_ref,
    own_ref,
    face_ref,
    corner_ref,
    off_ref,
    vv,
    rs,
    dg,
    wide,
    mb,
    sx,
    sy,
    zp,
    ab,
    vx,
    vy,
    rx,
    ry,
    rc,
    rr,
    vc,
    cb,
    cr,
    load_sem,
    send_sem,
    recv_sem,
    csend_sem,
    crecv_sem,
    relay_sem,
    across_sem,
    sum_out,
    sum_in,
    tell_sem,
):
    rows, c_x, c_y, c_z = vec_ref.shape
    direct = c_y * SHARE // 32
    chunk_rows = (c_y - direct) // 2
    pitch = c_y + 1
    ix, iy = lax.axis_index("sx"), lax.axis_index("sy")

    def guarded(there, action):
        @pl.when(there)
        def _():
            action()

    low_x, high_x = ix > 0, ix < n_x - 1
    low_y, high_y = iy > 0, iy < n_y - 1
    faces = [
        (low_x, (ix - 1, iy)),
        (high_x, (ix + 1, iy)),
        (low_y, (ix, iy - 1)),
        (high_y, (ix, iy + 1)),
    ]
    across_low, across_high = n_x // 2 - 1, n_x // 2

    def at_once(d):
        return (ix == (across_high, across_low)[d]) | (ix == (n_x - 2, n_x - 3)[d])

    def place(x):
        return (0, *range(2, c_x), 1)[x]

    def origin_of(d):
        return ix == (across_high, across_low)[d]

    def across(d, side):
        return faces[d][1][0], iy - 1 + 2 * side

    barrier = pltpu.get_barrier_semaphore()
    for there, device in faces:

        @pl.when(there)
        def _(device=device):
            pl.semaphore_signal(barrier, inc=1, device_id=device, device_id_type=MESH)

    mid = n_y // 2
    upper = iy >= mid
    slot = lax.rem(iy, mid)
    is_teller = iy == mid - 1
    for far in range(2, mid):

        @pl.when(slot >= far)
        def _(far=far):
            pl.semaphore_signal(barrier, inc=1, device_id=(ix, iy - far), device_id_type=MESH)

    @pl.when(iy > mid)
    def _():
        pl.semaphore_signal(barrier, inc=1, device_id=(ix, mid - 1), device_id_type=MESH)

    is_origin = (ix == across_low) | (ix == across_high)
    is_relay = (ix == 0) | (ix == n_x - 1)
    via_y = iy + 1 - 2 * lax.rem(iy, 2)
    origin_to = (jnp.where(ix == across_low, n_x - 1, 0), via_y)
    relay_to = (jnp.where(ix == 0, across_low, across_high), via_y)
    relay_from = (jnp.where(ix == 0, across_high, across_low), via_y)
    target_from = (jnp.where(ix == across_low, 0, n_x - 1), via_y)

    @pl.when(is_relay)
    def _():
        pl.semaphore_signal(barrier, inc=1, device_id=relay_from, device_id_type=MESH)

    @pl.when(is_origin)
    def _():
        pl.semaphore_signal(barrier, inc=1, device_id=target_from, device_id_type=MESH)

    def load(x):
        return pltpu.make_async_copy(vec_ref.at[:, x], vv.at[x], load_sem.at[x])

    rs_load = pltpu.make_async_copy(rs_ref, rs, load_sem.at[c_x])
    dg_load = pltpu.make_async_copy(dg_ref, dg, load_sem.at[c_x + 1])
    rs_load.start()
    load(0).start()
    load(c_x - 1).start()
    for x in range(1, c_x - 1):
        load(x).start()
    dg_load.start()

    greeted = sum(there.astype(jnp.int32) for there, _ in faces)
    greeted = greeted + (is_relay | is_origin).astype(jnp.int32)
    for side, there in enumerate((low_y, high_y)):
        for d in range(2):

            @pl.when(at_once(d) & there)
            def _(side=side, d=d):
                pl.semaphore_signal(barrier, inc=1, device_id=across(d, side), device_id_type=MESH)

        greeted = greeted + ((at_once(0) | at_once(1)) & there).astype(jnp.int32)
    greeted = greeted + jnp.maximum(mid - 2 - slot, 0)
    greeted = greeted + jnp.where(is_teller, n_y - mid - 1, 0)

    def zero_layers(ref):
        def step(i, _):
            ref[i] = jnp.zeros((rows, c_z), BF16)
            return _

        lax.fori_loop(0, ref.shape[0], step, 0)

    for d in range(4):
        layers = rx.at[d] if d < 2 else ry.at[d - 2]
        guarded(jnp.logical_not(faces[d][0]), lambda layers=layers: zero_layers(layers))

        if d < 2:

            @pl.when(jnp.logical_not(faces[d][0]))
            def _(d=d):
                rc[2 * d] = jnp.zeros((rows, c_z), BF16)
                rc[2 * d + 1] = jnp.zeros((rows, c_z), BF16)

            for side, there in enumerate((low_y, high_y)):

                @pl.when(at_once(d) & jnp.logical_not(there))
                def _(d=d, side=side):
                    rc[2 * d + side] = jnp.zeros((rows, c_z), BF16)

    lane_r = lax.broadcasted_iota(jnp.int32, (c_z, c_z), 0)
    lane_c = lax.broadcasted_iota(jnp.int32, (c_z, c_z), 1)
    apart = jnp.abs(lane_r - lane_c)
    smooth = jnp.where(apart == 0, 1.0, jnp.where(apart == 1, 0.5, 0.0)).astype(BF16)

    def zero_row(y, _):
        zp[0, y] = jnp.zeros((rows, c_z), F32)
        zp[c_x + 1, y] = jnp.zeros((rows, c_z), F32)
        return _

    lax.fori_loop(0, c_y + 2, zero_row, 0)
    for x in range(1, c_x + 1):
        zp[x, 0] = jnp.zeros((rows, c_z), F32)
        zp[x, c_y + 1] = jnp.zeros((rows, c_z), F32)

    count = cnt_ref[0, 0]
    cb[...] = jnp.full(cb.shape, count, jnp.int32)
    keep = lax.broadcasted_iota(jnp.int32, (rows, c_z), 0) < count

    def widen(x):
        load(x).wait()
        for a in range(rows):
            wide[x, a * pitch : a * pitch + c_y, :] = vv[x, a].astype(F32)

    def row(x, y):
        m = jnp.where(keep, wide[x, pl.ds(y, rows, stride=pitch), :], 0.0)
        return m, m * rs[x, y : y + 1, :]

    def smoothed(x, pieces):
        z = jnp.dot(jnp.concatenate(pieces, axis=0), smooth, preferred_element_type=F32)
        for y in range(c_y):
            zp[x + 1, y + 1] = z[y * rows : (y + 1) * rows]

    def scale(x):
        pieces = []
        for y in range(c_y):
            m, s = row(x, y)
            mb[x, y] = m.astype(BF16)
            pieces.append(s.astype(BF16))
        smoothed(x, pieces)

    rs_load.wait()
    for side, x in enumerate((0, c_x - 1)):
        widen(x)
        for y in range(c_y):
            m, s = row(x, y)
            mb[x, y] = m.astype(BF16)
            sx[side, y] = s.astype(BF16)

    def widen_step(x, _):
        widen(x)
        return _

    lax.fori_loop(1, c_x - 1, widen_step, 0)
    for x in range(c_x):
        sy[0, place(x)] = row(x, 0)[1].astype(BF16)
        sy[1, place(x)] = row(x, c_y - 1)[1].astype(BF16)

    pl.semaphore_wait(barrier, greeted)

    def to_face(d, part, to=None):
        opposite = d ^ 1
        if d < 2:
            piece = pl.ds(direct, c_y - direct) if part else pl.ds(0, direct)
            src, dst = sx.at[d, piece], rx.at[opposite, piece]
        else:
            piece = pl.ds(2, c_x - 2) if part else pl.ds(0, 2)
            src, dst = sy.at[d - 2, piece], ry.at[opposite - 2, piece]
        return pltpu.make_async_remote_copy(
            src_ref=src,
            dst_ref=dst,
            send_sem=send_sem.at[part * 4 + d],
            recv_sem=recv_sem.at[part * 4 + opposite],
            device_id=faces[d if to is None else to][1],
            device_id_type=MESH,
        )

    def from_face(d, part):
        return to_face(d ^ 1, part, d)

    def by_relay(d, leg, chunk):
        opposite = d ^ 1
        piece = pl.ds(direct + chunk * chunk_rows, chunk_rows)
        src, dst = [
            (sx.at[d, piece], rr.at[chunk]),
            (rr.at[chunk], rx.at[opposite, piece]),
        ][leg]
        return pltpu.make_async_remote_copy(
            src_ref=src,
            dst_ref=dst,
            send_sem=relay_sem.at[0, leg, chunk],
            recv_sem=relay_sem.at[1, leg, chunk],
            device_id=(origin_to, relay_to)[leg],
            device_id_type=MESH,
        )

    def to_corner(d, to=None):
        opposite = d ^ 1
        return pltpu.make_async_remote_copy(
            src_ref=ry.at[pl.ds(0, 2), d],
            dst_ref=rc.at[pl.ds(2 * opposite, 2)],
            send_sem=send_sem.at[8 + d],
            recv_sem=recv_sem.at[8 + opposite],
            device_id=faces[d if to is None else to][1],
            device_id_type=MESH,
        )

    def to_across(d, side, device=None):
        return pltpu.make_async_remote_copy(
            src_ref=sy.at[side, d],
            dst_ref=rc.at[2 * (d ^ 1) + 1 - side],
            send_sem=across_sem.at[0, side],
            recv_sem=across_sem.at[1, 1 - side],
            device_id=across(d, side) if device is None else device,
            device_id_type=MESH,
        )

    def from_across(d, side):
        return to_across(d ^ 1, 1 - side, across(d, side))

    def at_across(action):
        for side, there in enumerate((low_y, high_y)):
            for d in range(2):
                guarded(at_once(d) & there, lambda side=side, d=d: action(d, side))

    def from_corner(d):
        return to_corner(d ^ 1, d)

    def to_peer(far):
        return pltpu.make_async_remote_copy(
            src_ref=cb,
            dst_ref=cr.at[far],
            send_sem=csend_sem.at[far],
            recv_sem=crecv_sem.at[far],
            device_id=(ix, iy + far),
            device_id_type=MESH,
        )

    def onward(d):
        return faces[d][0] & jnp.logical_not(at_once(d))

    def send_x(d):
        @pl.when(origin_of(d))
        def _():
            for chunk in range(2):
                by_relay(d, 0, chunk).start()

        to_face(d, 0).start()

        @pl.when(jnp.logical_not(origin_of(d)))
        def _():
            to_face(d, 1).start()

    for far in range(1, mid):
        guarded(slot + far < mid, lambda far=far: to_peer(far).start())
    for d in (3, 2):
        guarded(faces[d][0], lambda d=d: to_face(d, 0).start())
    at_across(lambda d, side: to_across(d, side).start())
    for d in (1, 0):
        guarded(faces[d][0], lambda d=d: send_x(d))
    for d in (3, 2):
        guarded(faces[d][0], lambda d=d: to_face(d, 1).start())

    for side, x in enumerate((0, c_x - 1)):
        smoothed(x, [sx[side, y] for y in range(c_y)])

    def scale_step(x, _):
        scale(x)
        return _

    lax.fori_loop(1, c_x - 1, scale_step, 0)

    for side, x in enumerate((1, c_x)):
        for y in range(c_y):
            vx[side, y] = (
                -0.25 * ((zp[x, y] + zp[x, y + 2]) + 2.0 * zp[x, y + 1])
            ).astype(BF16)
    for side, y in enumerate((1, c_y)):
        for x in range(c_x):
            vy[side, place(x)] = (
                -0.25 * ((zp[x, y] + zp[x + 2, y]) + 2.0 * zp[x + 1, y])
            ).astype(BF16)

    dg_load.wait()
    dg[...] = dg[...] + rs[...] * rs[...]
    rs[...] = rs[...] * 0.25

    def apply(x, slot):
        def across(y):
            near = zp[x + 1, y]
            return (zp[x, y] + near) + (near + zp[x + 2, y])

        here = across(1)
        before = here
        for y in range(c_y):
            ahead = across(y + 2)
            after = here + ahead
            m = mb[x, y].astype(F32)
            applied = dg[x, pl.ds(y, 1), :] * m - rs[x, pl.ds(y, 1), :] * (before + after)
            ab[slot, y] = applied.astype(BF16)
            here, before = ahead, after

    def product(x, slot):
        return block_dot(mb.at[x], 0, ab.at[slot], 0, c_y)

    apply(0, 0)

    def own_step(i, total):
        x = 2 * i
        total = total + product(x, 0)
        apply(x + 1, 1)
        total = total + product(x + 1, 1)
        apply(x + 2, 0)
        return total

    def to_upper(other):
        return pltpu.make_async_remote_copy(
            src_ref=sum_out,
            dst_ref=sum_in,
            send_sem=tell_sem.at[other - mid],
            recv_sem=tell_sem.at[n_y - mid],
            device_id=(ix, other),
            device_id_type=MESH,
        )

    def add_counts():
        off_ref[...] = jnp.zeros(off_ref.shape, jnp.int32)
        for far in range(1, mid):

            def earlier(far=far):
                to_peer(far).wait_recv()
                off_ref[...] += cr[far]

            guarded(slot >= far, earlier)

        @pl.when(is_teller)
        def _():
            sum_out[...] = off_ref[...] + count
            for other in range(mid, n_y):
                to_upper(other).start()

    def hand_on_corners():
        for d in (2, 3):
            guarded(faces[d][0], lambda d=d: from_face(d, 0).wait_recv())
        for d in (0, 1):
            guarded(onward(d), lambda d=d: to_corner(d).start())

    def hand_over(d, chunk):
        by_relay(d, 0, chunk).wait_recv()
        by_relay(d, 1, chunk).start()

    total = jnp.zeros((rows, rows), F32)
    for step in range(c_x // 2 - 1):
        if step < 2:
            guarded(ix == 0, lambda step=step: hand_over(0, step))
            guarded(ix == n_x - 1, lambda step=step: hand_over(1, step))
        total = lax.fori_loop(step, step + 1, own_step, total)
        if step == 1:
            add_counts()
            hand_on_corners()
    total = total + product(c_x - 2, 0)
    apply(c_x - 1, 1)
    own_ref[0, 0] = total + product(c_x - 1, 1)

    for d in range(4):
        x, y = (0, c_x - 1)[d // 2], (0, c_y - 1)[d % 2]
        vc[d] = (-0.25 * zp[x + 1, y + 1]).astype(BF16)

    def rest_x(d):
        @pl.when(origin_of(d))
        def _():
            for chunk in range(2):
                by_relay(d ^ 1, 1, chunk).wait_recv()

        @pl.when(jnp.logical_not(origin_of(d)))
        def _():
            from_face(d, 1).wait_recv()

    for d in (0, 1):
        guarded(onward(d), lambda d=d: from_corner(d).wait_recv())
    at_across(lambda d, side: from_across(d, side).wait_recv())
    for d in (0, 1):
        guarded(faces[d][0], lambda d=d: from_face(d, 0).wait_recv())
    corner_ref[0, 0] = along_lanes([row_dot(vc[d], rc[d]) for d in range(4)])
    products = [block_dot(vx.at[d], 0, rx.at[d], 0, direct) for d in range(2)]
    face_ref[0, 0, :, 0 : 2 * rows] = along_lanes(products)
    for d in (2, 3):
        guarded(faces[d][0], lambda d=d: from_face(d, 1).wait_recv())
    for d in (0, 1):
        guarded(faces[d][0], lambda d=d: rest_x(d))
    products = [block_dot(vx.at[d], direct, rx.at[d], direct, c_y - direct) for d in range(2)]
    face_ref[0, 0, :, 0 : 2 * rows] += along_lanes(products)
    products = [block_dot(vy.at[d], 0, ry.at[d], 0, c_x) for d in range(2)]
    face_ref[0, 0, :, 2 * rows : 4 * rows] = along_lanes(products)

    @pl.when(upper)
    def _():
        to_upper(mid).wait_recv()
        off_ref[...] += sum_in[...]

    def sent(d):
        to_face(d, 0).wait_send()
        if d >= 2:
            to_face(d, 1).wait_send()
        else:
            guarded(onward(d), lambda: to_corner(d).wait_send())

            @pl.when(origin_of(d))
            def _():
                for chunk in range(2):
                    by_relay(d, 0, chunk).wait_send()

            @pl.when(jnp.logical_not(origin_of(d)))
            def _():
                to_face(d, 1).wait_send()

    for d in range(4):
        guarded(faces[d][0], lambda d=d: sent(d))
    at_across(lambda d, side: to_across(d, side).wait_send())

    @pl.when(is_relay)
    def _():
        for chunk in range(2):
            by_relay(0, 1, chunk).wait_send()

    for far in range(1, mid):
        guarded(slot + far < mid, lambda far=far: to_peer(far).wait_send())

    @pl.when(is_teller)
    def _():
        for other in range(mid, n_y):
            to_upper(other).wait_send()


def hand_on(own_in, face_in, corner_in, off_in, own_out, face_out, corner_out, off_out, wide, first, sems):
    pairs = [(off_in, wide), (face_in, face_out), (corner_in, corner_out), (own_in, own_out)]
    copies = [pltpu.make_async_copy(a, b, sems.at[i]) for i, (a, b) in enumerate(pairs)]
    for copy in copies:
        copy.start()
    copies[0].wait()
    first[...] = wide[0:1, 0:1]
    last = pltpu.make_async_copy(first, off_out, sems.at[len(pairs)])
    last.start()
    for copy in copies[1:]:
        copy.wait()
    last.wait()


def on_device(n_x, n_y, vectors, root_stiff, diag_coef, counts):
    rows, c_x, c_y, c_z = vectors.shape
    vmem = pltpu.VMEM
    results = (
        jax.ShapeDtypeStruct((1, 1, rows, rows), F32),
        jax.ShapeDtypeStruct((1, 1, rows, 4 * rows), F32),
        jax.ShapeDtypeStruct((1, 1, rows, 4 * rows), F32),
        jax.ShapeDtypeStruct((1, 1), jnp.int32),
    )
    anywhere = pl.BlockSpec(memory_space=pl.ANY)
    outputs = pl.pallas_call(
        functools.partial(kernel, n_x, n_y),
        out_shape=results[:3] + (jax.ShapeDtypeStruct((8, c_z), jnp.int32),),
        in_specs=[anywhere] * 3 + [pl.BlockSpec(memory_space=pltpu.SMEM)],
        out_specs=[pl.BlockSpec(memory_space=vmem)] * 4,
        scratch_shapes=[
            vmem((c_x, rows, c_y, c_z), BF16),
            vmem((c_x, c_y, c_z), F32),
            vmem((c_x, c_y, c_z), F32),
            vmem((c_x, rows * (c_y + 1) + 7, c_z), F32),
            vmem((c_x, c_y, rows, c_z), BF16),
            vmem((2, c_y, rows, c_z), BF16),
            vmem((2, c_x, rows, c_z), BF16),
            vmem((c_x + 2, c_y + 2, rows, c_z), F32),
            vmem((2, c_y, rows, c_z), BF16),
            vmem((2, c_y, rows, c_z), BF16),
            vmem((2, c_x, rows, c_z), BF16),
            vmem((2, c_y, rows, c_z), BF16),
            vmem((2, c_x, rows, c_z), BF16),
            vmem((4, rows, c_z), BF16),
            vmem((2, (c_y - c_y * SHARE // 32) // 2, rows, c_z), BF16),
            vmem((4, rows, c_z), BF16),
            vmem((8, c_z), jnp.int32),
            vmem((n_y, 8, c_z), jnp.int32),
            pltpu.SemaphoreType.DMA((c_x + 2,)),
            pltpu.SemaphoreType.DMA((12,)),
            pltpu.SemaphoreType.DMA((12,)),
            pltpu.SemaphoreType.DMA((n_y,)),
            pltpu.SemaphoreType.DMA((n_y,)),
            pltpu.SemaphoreType.DMA((2, 2, 2)),
            pltpu.SemaphoreType.DMA((2, 2)),
            vmem((8, c_z), jnp.int32),
            vmem((8, c_z), jnp.int32),
            pltpu.SemaphoreType.DMA((n_y - n_y // 2 + 1,)),
        ],
        compiler_params=pltpu.CompilerParams(
            collective_id=0, has_side_effects=True, vmem_limit_bytes=55040 * 1024
        ),
        cost_estimate=pl.CostEstimate(flops=600_000_000, bytes_accessed=5_000_000, transcendentals=0),
        name="coarse",
    )(vectors, root_stiff, diag_coef, counts)
    return pl.pallas_call(
        hand_on,
        out_shape=results,
        in_specs=[anywhere] * 4,
        out_specs=[anywhere] * 4,
        scratch_shapes=[
            vmem((8, c_z), jnp.int32),
            vmem((1, 1), jnp.int32),
            pltpu.SemaphoreType.DMA((5,)),
        ],
        name="results",
        compiler_params=pltpu.CompilerParams(vmem_limit_bytes=4 * 1024 * 1024),
    )(*outputs)


def solution(mesh):
    n_x, n_y = mesh.shape["sx"], mesh.shape["sy"]
    return jax.shard_map(
        functools.partial(on_device, n_x, n_y),
        mesh=mesh,
        in_specs=(
            P(None, "sx", "sy", None),
            P("sx", "sy", None),
            P("sx", "sy", None),
            P("sx", "sy"),
        ),
        out_specs=(
            P("sx", "sy", None, None),
            P("sx", "sy", None, None),
            P("sx", "sy", None, None),
            P("sx", "sy"),
        ),
        check_vma=False,
    )
```
